512 devices in a mesh: mode: 8 (over y, core), pb: 64 (over x, z).
Axes of the slice: x: 4, y: 4, z: 16, core: 2. Of those that a mesh axis runs over, the one named last changes fastest.
Arguments:
- g_wann: bfloat16 [256, 2, 144, 1024], P('pb', None, 'mode'), may hold values from -0.25 to 0.25
- rot_k: bfloat16 [2, 32, 8], replicated, may hold values from -1 to 1
- qpoints: int32 [3, 4096], P(None, 'pb'), may hold values from 0 to 31
- rot_kq: bfloat16 [4096, 2, 32, 32], P('pb'), may hold values from -1 to 1
- win_count: int32 [512], P('pb'), may hold values from 1 to 16, as said below
- win_start: int32 [512], P('pb'), may hold values from 0 to 16, as said below
- modes_vec: bfloat16 [4096, 2, 144, 144], P('pb', None, 'mode'), may hold values from -0.5 to 0.5
- frequencies: float32 [4096, 144], P('pb', 'mode'), may hold values from 0.5 to 4
Outputs:
- coupling: bfloat16 [4096, 2, 144, 128], P('pb', None, 'mode')
The draws below stay inside these ranges and needn't reach their ends.
Inputs may be any that keep to these rules, and one draw needn't show every extreme that they name: `win_count`: each entry belongs to 8 consecutive q points; some block has exactly 16 bands. `win_start`: some block starts at 16.
All inputs are finite; a program needn't handle non-finite values.
Results may differ from the reference program's by a relative error of at most 0.0067.
Values may be sent and summed in bfloat16 or wider, within the bound.
A program may use at most 64 MiB of HBM per device.

```python
import math
import jax
import jax.numpy as jnp
from jax import lax

NW = 32
NCART = 144
NBK = 8
NBW = 16
GRID = 32
QB = 8
Q_DEV = 64
NQ = 4096
NR = 256
N_PB = 64


def draw_win_count(key, part):
    block_total = NQ // QB
    counts = jax.random.randint(key, (block_total,), 1, NBW + 1, dtype=jnp.int32)
    where_most = jax.random.randint(jax.random.fold_in(key, 11), (), 0, block_total, dtype=jnp.int32)
    return counts.at[where_most].set(NBW)


def draw_win_start(key, part):
    block_total = NQ // QB
    starts = jax.random.randint(key, (block_total,), 0, NW - NBW + 1, dtype=jnp.int32)
    where_most = jax.random.randint(jax.random.fold_in(key, 23), (), 0, block_total, dtype=jnp.int32)
    return starts.at[where_most].set(NW - NBW)


def set_ends(values, stream_key, least, high):
    shape = values.shape
    spot = [jax.random.randint(jax.random.fold_in(stream_key, axis), (), 0, shape[axis]) for axis in range(len(shape))]
    values = values.at[tuple(spot)].set(least)
    longest = shape.index(max(shape))
    spot[longest] = (spot[longest] + 1) % shape[longest]
    return values.at[tuple(spot)].set(high)


def levels(own_key, shape, pieces, smallest, largest):
    level = 1.0
    for axis_at, shards_of in pieces:
        heights = jax.random.uniform(jax.random.fold_in(jax.random.fold_in(own_key, 6), axis_at), (shards_of,), jnp.float32, smallest / len(pieces), largest / len(pieces))
        level = level * jnp.repeat(jnp.exp(heights), shape[axis_at] // shards_of).reshape((-1,) + (1,) * (len(shape) - 1 - axis_at))
    return level


def scatter_about(key, dims, width, reach, pieces=(), kind=jnp.bfloat16):
    array = width * jax.random.normal(key, dims, jnp.float32)
    if pieces:
        array = array * levels(key, dims, pieces, -0.22, 0.18)
    return jnp.clip(array, -reach, reach).astype(kind)


def setup_inputs(seed: int = 0) -> dict:
    keys = jax.random.split(jax.random.key(seed), 9)
    return {
        "g_wann": scatter_about(keys[0], (NR, 2, NCART, NW * NW), (2 * NR) ** -0.5, 0.25, ((0, 64), (2, 8))),
        "rot_k": scatter_about(keys[1], (2, NW, NBK), NW ** -0.5, 1.0),
        "qpoints": set_ends(jax.random.randint(keys[2], (3, NQ), 0, GRID), jax.random.fold_in(keys[2], 1), 0, GRID - 1).astype(jnp.int32),
        "rot_kq": scatter_about(keys[3], (NQ, 2, NW, NW), NW ** -0.5, 1.0, ((0, 64),)),
        "win_count": draw_win_count(jax.random.fold_in(keys[8], 71), 0),
        "win_start": draw_win_start(jax.random.fold_in(keys[8], 71), 0),
        "modes_vec": scatter_about(keys[6], (NQ, 2, NCART, NCART), NCART ** -0.5, 0.5, ((0, 64), (2, 8))),
        "frequencies": jnp.clip(jnp.exp(math.log(4.0) - 2.0794415 * jax.random.uniform(keys[7], (NQ, NCART), jnp.float32) ** levels(keys[7], (NQ, NCART), ((0, 64), (1, 8)), -0.2, 0.2)), 0.5, 4.0),
    }


two_pi = 6.283185307179586

def lattice_coords(cell_index):
    along_x = cell_index % 8 - 4
    along_y = cell_index // 8 % 8 - 4
    along_z = cell_index // 64 - 4
    return (along_x, along_y, along_z)

def phase_sum(q_coords, r_index, k_flat, col_width):
    along_x, along_y, along_z = lattice_coords(r_index)
    inner_sum = q_coords[0][:, None] * along_x[None, :] + q_coords[1][:, None] * along_y[None, :] + q_coords[2][:, None] * along_z[None, :]
    folded = jnp.mod(inner_sum, GRID)
    angles = folded.astype(jnp.float32) * (two_pi / GRID)
    cos_part = jnp.cos(angles).astype(jnp.bfloat16)
    sin_part = jnp.sin(angles).astype(jnp.bfloat16)
    row_count = cos_part.shape[0]
    stacked = jnp.concatenate([cos_part, sin_part], axis=0)
    product = jnp.dot(stacked, k_flat, preferred_element_type=jnp.float32)
    real_part = product[:row_count, :col_width] - product[row_count:, col_width:]
    imag_part = product[:row_count, col_width:] + product[row_count:, :col_width]
    return jnp.stack([real_part, imag_part], axis=1).astype(jnp.bfloat16)

def reference(g_wann, rot_k, qpoints, rot_kq, win_count, win_start, modes_vec, frequencies):
    r_total = g_wann.shape[0]
    wannier = g_wann.astype(jnp.float32).reshape(r_total, 2, NCART, NW, NW)
    rot_float = rot_k.astype(jnp.float32)

    def rotate_k(first_op, second_op):
        return jnp.einsum('rcij,jb->rcib', first_op, second_op)
    k_real = rotate_k(wannier[:, 0], rot_float[0]) - rotate_k(wannier[:, 1], rot_float[1])
    k_imag = rotate_k(wannier[:, 0], rot_float[1]) + rotate_k(wannier[:, 1], rot_float[0])
    k_side = jnp.stack([k_real, k_imag], axis=1).astype(jnp.bfloat16).reshape(r_total, 2 * NCART * NW * NBK)
    col_width = NCART * NW * NBK
    r_index = jnp.arange(r_total, dtype=jnp.int32)
    slot_index = jnp.arange(NBW, dtype=jnp.int32)
    per_block = Q_DEV // QB

    def one_block(block_index):
        q_coords = lax.dynamic_slice_in_dim(qpoints, block_index * Q_DEV, Q_DEV, 1)
        q_sum = phase_sum(q_coords, r_index, k_side, col_width)
        q_sum = lax.optimization_barrier(q_sum).astype(jnp.float32).reshape(Q_DEV, 2, NCART, NW, NBK)
        counts_q = jnp.repeat(lax.dynamic_slice_in_dim(win_count, block_index * per_block, per_block, 0), QB, total_repeat_length=Q_DEV)
        starts_q = jnp.repeat(lax.dynamic_slice_in_dim(win_start, block_index * per_block, per_block, 0), QB, total_repeat_length=Q_DEV)
        lifted = lax.dynamic_slice_in_dim(rot_kq, block_index * Q_DEV, Q_DEV, 0).astype(jnp.float32)
        picks = (starts_q[:, None] + slot_index[None, :]).astype(jnp.int32)
        window = jnp.take_along_axis(lifted, jnp.broadcast_to(picks[:, None, None, :], (Q_DEV, 2, NW, NBW)), axis=3)
        live = (slot_index[None, :] < counts_q[:, None]).astype(jnp.float32)
        window = window * live[:, None, None, :]

        def rotate_band(first_op, second_op):
            return jnp.einsum('qim,qcib->qcmb', first_op, second_op)
        band_real = rotate_band(window[:, 0], q_sum[:, 0]) + rotate_band(window[:, 1], q_sum[:, 1])
        band_imag = rotate_band(window[:, 0], q_sum[:, 1]) - rotate_band(window[:, 1], q_sum[:, 0])
        band_blocks = jnp.stack([band_real, band_imag], axis=1).astype(jnp.bfloat16)
        band_blocks = lax.optimization_barrier(band_blocks).astype(jnp.float32).reshape(Q_DEV, 2, NCART, NBW * NBK)
        vectors = lax.dynamic_slice_in_dim(modes_vec, block_index * Q_DEV, Q_DEV, 0).astype(jnp.float32)

        def contract(first_op, second_op):
            return jnp.einsum('qvc,qcx->qvx', first_op, second_op)
        out_real = contract(vectors[:, 0], band_blocks[:, 0]) - contract(vectors[:, 1], band_blocks[:, 1])
        out_imag = contract(vectors[:, 0], band_blocks[:, 1]) + contract(vectors[:, 1], band_blocks[:, 0])
        freq_block = lax.dynamic_slice_in_dim(frequencies, block_index * Q_DEV, Q_DEV, 0)
        mode_scale = 1.0 / jnp.sqrt(2.0 * freq_block)
        rotated = jnp.stack([out_real, out_imag], axis=1) * mode_scale[:, None, :, None]
        return rotated.astype(jnp.bfloat16)
    blocks_out = lax.map(one_block, jnp.arange(N_PB, dtype=jnp.int32))
    return blocks_out.reshape(Q_DEV * N_PB, 2, NCART, NBW * NBK)
```

```python
import functools
import jax
import jax.numpy as jnp
import numpy as np
from jax import lax
from jax.experimental import pallas as pl
from jax.experimental.pallas import tpu as pltpu
from jax.sharding import PartitionSpec as P

NX = 4
NM = 8
TWO_PI = 6.283185307179586
BF = jnp.bfloat16
F32 = jnp.float32


def dot(a, b):
    return jnp.dot(a, b, preferred_element_type=F32)


def constants(nz):
    rows = np.arange(nz * 16)
    z, x, r4 = rows // 16, rows // 4 % 4, rows % 4
    r = (x * nz + z) * 4 + r4
    lattice = np.zeros((128, nz * 16), np.float32)
    lattice[0] = r % 8 - 4
    lattice[1] = r // 8 % 8 - 4
    lattice[2] = r // 64 - 4

    row, lane = np.arange(256)[:, None], np.arange(128)[None, :]
    same = row // 32 == lane // 16
    shift = np.where(same, row % 32 - lane % 16, -1000).astype(np.int32)

    spread = np.zeros((2, 4, 2, 16, 4, 2, 2, 2, 2, 16, 2), np.float32)
    for par in range(2):
        for q4 in range(4):
            for m in range(16):
                for b in range(2):
                    spread[par, q4, 0, m, q4, 0, b, par, 0, m, b] = 1
                    spread[par, q4, 1, m, q4, 1, b, par, 0, m, b] = 1
                    spread[par, q4, 1, m, q4, 0, b, par, 1, m, b] = -1
                    spread[par, q4, 0, m, q4, 1, b, par, 1, m, b] = 1
    spread = spread.reshape(2, 128, 2048)

    pick = np.zeros((384, 1536), np.float32)
    for ri in range(2):
        for c in range(144):
            source = ri * 128 + c if c < 128 else 256 + ri * 16 + c - 128
            for q4 in range(4):
                pick[source, ri * 640 + c // 18 * 80 + q4 * 20 + c % 18] = 1
    pick[288:291, 1280:] = 1
    mask = np.zeros((2, 2, 4, 18, 8, 4, 20), np.float32)
    for par in range(2):
        for q4 in range(4):
            mask[par, par, q4, :, :, q4, :] = 1
    mask = mask.reshape(2, 144, 640)

    order = np.zeros((4, 2, 2, 16, 2, 2, 2, 2, 16, 8), np.float32)
    for xx in range(4):
        for par in range(2):
            for m in range(16):
                for b in range(2):
                    order[xx, par, 0, m, b, par, 0, 0, m, xx * 2 + b] = 1
                    order[xx, par, 1, m, b, par, 0, 1, m, xx * 2 + b] = 1
                    order[xx, par, 1, m, b, par, 1, 0, m, xx * 2 + b] = -1
                    order[xx, par, 0, m, b, par, 1, 1, m, xx * 2 + b] = 1
    order = order.reshape(512, 1024)
    half = lambda a: jnp.asarray(a, BF)
    return half(lattice), jnp.asarray(shift), half(spread), half(pick), half(mask), half(order)


def kernel(
    nz, ws_ref, wc_ref, g_ref, base_ref, qm_ref, rotq_ref, modes_ref,
    lattice_ref, shift_ref, spread_ref, pick_ref, mask_ref, order_ref, o_ref,
    gl, kw, kf, ksend, krecv, kx, ka, kbuf, ph, win, wq, qbuf, bsend, brecv, mrecv, lhs, scale, rhs, osend,
    ks_sem, kr_sem, ps_sem, pr_sem, ns_sem, nr_sem, ms_sem, mr_sem, zs_sem, zr_sem, bs_sem, br_sem, os_sem, or_sem,
):
    me = lax.axis_index("mode")
    pb = lax.axis_index("pb")
    x, z = pb // nz, pb % nz
    nr = nz * 16

    def at(xx, mm):
        return {"mode": mm, "pb": xx * nz + z}

    def remote(src, dst, ssem, rsem, where):
        return pltpu.make_async_remote_copy(
            src_ref=src, dst_ref=dst, send_sem=ssem, recv_sem=rsem,
            device_id=where, device_id_type=pl.DeviceIdType.MESH,
        )

    right = {"mode": me, "pb": x * nz + (z + 1) % nz}
    left = {"mode": me, "pb": x * nz + (z + nz - 1) % nz}

    barrier = pltpu.get_barrier_semaphore()

    @pl.loop(1, 32)
    def _(d):
        pl.semaphore_signal(
            barrier, inc=1, device_id=at((x + d // 8) % 4, (me + d) % 8), device_id_type=pl.DeviceIdType.MESH
        )

    if nz > 1:
        pl.semaphore_signal(barrier, inc=1, device_id=left, device_id_type=pl.DeviceIdType.MESH)
        pl.semaphore_signal(barrier, inc=1, device_id=right, device_id_type=pl.DeviceIdType.MESH)

    lane_i = lax.broadcasted_iota(jnp.int32, (32, 512), 1) % 32
    for ri in range(2):
        part = base_ref[ri * 32:(ri + 1) * 32, :]

        @pl.loop(0, 32)
        def _(i):
            kw[pl.ds(pl.multiple_of(ri * 1024 + i * 32, 32), 32), :] = jnp.where(lane_i == i, part, 0.0).astype(BF)

    for r in range(4):
        for ri in range(2):
            gl[r * 32:r * 32 + 18, ri * 1024:(ri + 1) * 1024] = g_ref[r, ri]
    turned = dot(gl[...], kw[...])
    kf[...] = jnp.zeros_like(kf)
    for xx in range(4):
        for r in range(4):
            kf[xx, pl.ds(r, 18, stride=4), :] = turned[r * 32:r * 32 + 18, xx * 128:(xx + 1) * 128]
    ksend[...] = kf[...].astype(BF)

    pl.semaphore_wait(barrier, 31 + (2 if nz > 1 else 0))

    for d in range(1, 4):
        xx = (x + d) % 4
        remote(ksend.at[xx], krecv.at[x], ks_sem.at[xx], kr_sem.at[x], at(xx, me)).start()
    krecv[x] = ksend[x]

    inner = dot(qm_ref[...], lattice_ref[...]).astype(jnp.int32) & 31
    angle = inner.astype(F32) * (TWO_PI / 32)
    ph[x, 0:64, :] = jnp.cos(angle).astype(BF)
    ph[x, 64:128, :] = jnp.sin(angle).astype(BF)
    for d in range(1, 4):
        xx = (x + d) % 4
        remote(ph.at[x], ph.at[x], ps_sem.at[xx], pr_sem.at[x], at(xx, me)).start()

    for d in range(1, 8):
        mm = (me + d) % 8
        remote(modes_ref.at[mm], mrecv.at[me], ms_sem.at[mm], mr_sem.at[me], at(x, mm)).start()
    mrecv[me] = modes_ref[me]

    lane_m = lax.broadcasted_iota(jnp.int32, (256, 128), 1) % 16
    for t in range(8):
        chosen = jnp.where((shift_ref[...] == ws_ref[t]) & (lane_m < wc_ref[t]), 1.0, 0.0).astype(BF)
        cut = dot(rotq_ref[t], chosen).astype(BF)
        win[x, 0, t * 32:(t + 1) * 32, :] = cut[0:32]
        win[x, 1, t * 32:(t + 1) * 32, :] = cut[32:64]
    for d in range(1, 4):
        xx = (x + d) % 4
        remote(win.at[x], win.at[x], ns_sem.at[xx], nr_sem.at[x], at(xx, me)).start()

    for d in range(1, 4):
        xx = (x + d) % 4
        remote(ksend.at[xx], krecv.at[xx], ks_sem.at[xx], kr_sem.at[xx], at(xx, me)).wait_recv()
    kx[...] = krecv[...].astype(F32)
    for xx in range(4):
        for r in range(4):
            ka[pl.ds(xx * 4 + r, 18, stride=16), :] = kx[xx, pl.ds(r, 18, stride=4), :]
    kbuf[z] = ka[...].astype(BF)

    def hop(way, step, part):
        shard = (z + (nz - step if way == 0 else step)) % nz
        piece = kbuf.at[shard, pl.ds(part * 144, 144)]
        return remote(piece, piece, zs_sem.at[way, step, part], zr_sem.at[way, step, part], right if way == 0 else left)

    hops = (nz // 2, nz - 1 - nz // 2)

    def weights(xx):
        for par in range(2):
            for q4 in range(4):
                spreaded = dot(win[xx, par], spread_ref[par, :, q4 * 512:(q4 + 1) * 512]).astype(BF)
                for g in range(4):
                    rows = spreaded[:, g * 128:(g + 1) * 128].reshape(8, 32, 128)
                    start = par * 128 + g * 32
                    wq[pl.ds(xx * 8, 8), q4, start:start + 32, :] = rows

    def vectors(mm):
        spreaded = dot(mrecv[mm], pick_ref[...])
        scale[mm] = spreaded[:, 1280:]
        both = spreaded[:, :1280].astype(BF)
        for par in range(2):
            for ri in range(2):
                start = (par * 2 + ri) * 640
                lhs[mm, :, start:start + 640] = both[:, ri * 640:(ri + 1) * 640] * mask_ref[par]

    def wait_window(xx):
        remote(win.at[xx], win.at[xx], ns_sem.at[xx], nr_sem.at[xx], at(xx, me)).wait_recv()

    def wait_vectors(mm):
        remote(modes_ref.at[mm], mrecv.at[mm], ms_sem.at[mm], mr_sem.at[mm], at(x, mm)).wait_recv()

    for step in range(8):
        for part in range(2):
            for way in range(2):
                if step < hops[way]:
                    if step > 0:
                        hop(way, step - 1, part).wait_recv()
                    hop(way, step, part).start()
        if step < 4:
            xx = (x + step) % 4
            if step > 0:
                wait_window(xx)
            weights(xx)
        mm = (me + step) % 8
        if step > 0:
            wait_vectors(mm)
        vectors(mm)
    for way in range(2):
        if hops[way]:
            for part in range(2):
                hop(way, hops[way] - 1, part).wait_recv()

    for d in range(1, 4):
        xx = (x + d) % 4
        remote(ph.at[xx], ph.at[xx], ps_sem.at[xx], pr_sem.at[xx], at(xx, me)).wait_recv()
    qbuf[...] = jnp.zeros_like(qbuf)
    turn = lax.broadcasted_iota(jnp.int32, (64, 128), 1) < 64

    @pl.loop(0, 9)
    def _(cp):
        pair = [
            kbuf[:, pl.ds(pl.multiple_of((cp * 2 + p) * 16, 16), 16), :].reshape(nr, 128) for p in range(2)
        ]
        both = dot(ph[...].reshape(512, nr), jnp.concatenate(pair, axis=1))
        for p in range(2):
            for xx in range(4):
                along = both[xx * 128:xx * 128 + 64, p * 128:(p + 1) * 128]
                across = pltpu.roll(both[xx * 128 + 64:xx * 128 + 128, p * 128:(p + 1) * 128], 64, 1)
                total = along + jnp.where(turn, -across, across)
                for par in range(2):
                    qbuf[par, pl.ds(xx * 640 + cp * 2 + p, 32, stride=20), :] = total[par * 32:(par + 1) * 32]

    row = lax.broadcasted_iota(jnp.int32, (80, 256), 0)

    def band(xx, mm):
        spot = xx * 8 + mm
        rows = pl.ds(pl.multiple_of(spot * 80, 80), 80)
        own = jnp.concatenate([qbuf[0, rows, :], qbuf[1, rows, :]], axis=1)
        wide = [
            jnp.where((row >= q4 * 20) & (row < q4 * 20 + 20), own, 0.0).astype(BF) for q4 in range(4)
        ]
        return dot(jnp.concatenate(wide, axis=1), wq[spot].reshape(1024, 128)).astype(BF)

    def block(xx, mm, sx, sm):
        return remote(
            bsend.at[xx * 8 + mm], brecv.at[sx, sm], bs_sem.at[xx * 8 + mm], br_sem.at[sx * 8 + sm], at(xx, mm)
        )

    @pl.loop(1, 32)
    def _(d):
        xx, mm = (x + d // 8) % 4, (me + d) % 8
        bsend[xx * 8 + mm] = band(xx, mm)
        block(xx, mm, x, me).start()

    brecv[x, me] = band(x, me)

    @pl.loop(1, 32)
    def _(d):
        xx, mm = (x + d // 8) % 4, (me + d) % 8
        block(xx, mm, xx, mm).wait_recv()

    blocks = jnp.concatenate([brecv[xx].reshape(640, 128) for xx in range(4)], axis=1)
    for part in range(4):
        rhs[part * 640:(part + 1) * 640, :] = dot(blocks, order_ref[:, part * 256:(part + 1) * 256]).astype(BF)

    def finish(mm):
        return (dot(lhs[mm], rhs[...]) * scale[mm]).astype(BF)

    @pl.loop(1, 8)
    def _(d):
        mm = (me + d) % 8
        osend[mm] = finish(mm)
        remote(osend.at[mm], o_ref.at[me], os_sem.at[mm], or_sem.at[me], at(x, mm)).start()

    o_ref[me] = finish(me)

    @pl.loop(1, 8)
    def _(d):
        mm = (me + d) % 8
        remote(osend.at[mm], o_ref.at[mm], os_sem.at[mm], or_sem.at[mm], at(x, mm)).wait()

    for d in range(1, 4):
        xx = (x + d) % 4
        remote(ksend.at[xx], krecv.at[x], ks_sem.at[xx], kr_sem.at[x], at(xx, me)).wait_send()
        remote(ph.at[x], ph.at[x], ps_sem.at[xx], pr_sem.at[x], at(xx, me)).wait_send()
        remote(win.at[x], win.at[x], ns_sem.at[xx], nr_sem.at[x], at(xx, me)).wait_send()
    for d in range(1, 8):
        mm = (me + d) % 8
        remote(modes_ref.at[mm], mrecv.at[me], ms_sem.at[mm], mr_sem.at[me], at(x, mm)).wait_send()
    for way in range(2):
        for step in range(hops[way]):
            for part in range(2):
                hop(way, step, part).wait_send()

    @pl.loop(1, 32)
    def _(d):
        xx, mm = (x + d // 8) % 4, (me + d) % 8
        block(xx, mm, x, me).wait_send()


def shards(g_wann, rot_k, qpoints, rot_kq, win_count, win_start, modes_vec, frequencies):
    nz = lax.axis_size("pb") // NX
    lattice, shift, spread, pick, mask, order = constants(nz)

    signs = jnp.stack([jnp.stack([rot_k[0], rot_k[1]], 1), jnp.stack([-rot_k[1], rot_k[0]], 1)])
    base = signs.reshape(2, 32, 2, 4, 2).transpose(0, 1, 3, 2, 4)
    base = jnp.broadcast_to(base[..., None], (2, 32, 4, 2, 2, 32)).reshape(64, 512)

    qm = qpoints.reshape(3, 8, 2, 4).transpose(2, 1, 3, 0).reshape(64, 3).astype(BF)
    qm = jnp.pad(qm, ((0, 0), (0, 125)))

    rotq = rot_kq.reshape(8, 2, 4, 2, 32, 32).transpose(0, 1, 4, 2, 3, 5).reshape(8, 64, 256)

    own = 1.0 / jnp.sqrt(2.0 * frequencies)
    high = lax.reduce_precision(own, 8, 7)
    middle = lax.reduce_precision(own - high, 8, 7)
    low = own - high - middle
    parts = jnp.stack([high, middle, low], axis=-1).astype(BF)
    modes = jnp.concatenate(
        [
            modes_vec[:, 0, :, :128], modes_vec[:, 1, :, :128],
            modes_vec[:, 0, :, 128:], modes_vec[:, 1, :, 128:], parts,
            jnp.zeros((64, 18, 93), BF),
        ],
        axis=-1,
    ).reshape(8, 144, 384)

    vmem = pl.BlockSpec(memory_space=pltpu.VMEM)
    smem = pl.BlockSpec(memory_space=pltpu.SMEM)
    sem = pltpu.SemaphoreType.DMA
    out = pl.pallas_call(
        functools.partial(kernel, nz),
        out_shape=jax.ShapeDtypeStruct((8, 144, 256), BF),
        in_specs=[smem, smem] + [vmem] * 11,
        out_specs=vmem,
        scratch_shapes=[
            pltpu.VMEM((128, 2048), BF),
            pltpu.VMEM((2048, 512), BF),
            pltpu.VMEM((4, 80, 128), F32),
            pltpu.VMEM((4, 80, 128), BF),
            pltpu.VMEM((4, 80, 128), BF),
            pltpu.VMEM((4, 80, 128), F32),
            pltpu.VMEM((288, 128), F32),
            pltpu.VMEM((nz, 288, 128), BF),
            pltpu.VMEM((4, 128, nz * 16), BF),
            pltpu.VMEM((4, 2, 256, 128), BF),
            pltpu.VMEM((32, 4, 256, 128), BF),
            pltpu.VMEM((2, 2560, 128), F32),
            pltpu.VMEM((32, 80, 128), BF),
            pltpu.VMEM((4, 8, 80, 128), BF),
            pltpu.VMEM((8, 144, 384), BF),
            pltpu.VMEM((8, 144, 2560), BF),
            pltpu.VMEM((8, 144, 256), F32),
            pltpu.VMEM((2560, 256), BF),
            pltpu.VMEM((8, 144, 256), BF),
            sem((4,)), sem((4,)), sem((4,)), sem((4,)), sem((4,)), sem((4,)), sem((8,)), sem((8,)),
            sem((2, 8, 2)), sem((2, 8, 2)), sem((32,)), sem((32,)), sem((8,)), sem((8,)),
        ],
        compiler_params=pltpu.CompilerParams(
            collective_id=0, has_side_effects=True, vmem_limit_bytes=56 * 1024 * 1024
        ),
    )(win_start, win_count, g_wann, base, qm, rotq, modes, lattice, shift, spread, pick, mask, order)
    return out.reshape(64, 18, 2, 128).transpose(0, 2, 1, 3)


def solution(mesh):
    placed = (
        P("pb", None, "mode", None),
        P(),
        P(None, "pb"),
        P("pb", None, None, None),
        P("pb"),
        P("pb"),
        P("pb", None, "mode", None),
        P("pb", "mode"),
    )
    return jax.shard_map(
        shards, mesh=mesh, in_specs=placed, out_specs=P("pb", None, "mode", None), check_vma=False
    )
```

```python
import functools
import jax
import jax.numpy as jnp
import numpy as np
from jax import lax
from jax.experimental import pallas as pl
from jax.experimental.pallas import tpu as pltpu
from jax.sharding import PartitionSpec as P

NX = 4
NM = 8
PARTS = 3
TWO_PI = 6.283185307179586
BF = jnp.bfloat16
F32 = jnp.float32


def dot(a, b):
    return jnp.dot(a, b, preferred_element_type=F32)


def dot_t(a, b):
    return lax.dot_general(a, b, (((1,), (1,)), ((), ())), preferred_element_type=F32)


def constants(nz):
    rows = np.arange(nz * 16)
    z, x, r4 = rows // 16, rows // 4 % 4, rows % 4
    r = (x * nz + z) * 4 + r4
    lattice = np.zeros((128, nz * 16), np.float32)
    lattice[0] = r % 8 - 4
    lattice[1] = r // 8 % 8 - 4
    lattice[2] = r // 64 - 4

    row, lane = np.arange(256)[:, None], np.arange(128)[None, :]
    same = row // 32 == lane // 16
    shift = np.where(same, row % 32 - lane % 16, -1000).astype(np.int32)

    spread = np.zeros((2, 4, 2, 16, 4, 2, 2, 2, 2, 16, 2), np.float32)
    for par in range(2):
        for q4 in range(4):
            for m in range(16):
                for b in range(2):
                    spread[par, q4, 0, m, q4, 0, b, par, 0, m, b] = 1
                    spread[par, q4, 1, m, q4, 1, b, par, 0, m, b] = 1
                    spread[par, q4, 1, m, q4, 0, b, par, 1, m, b] = -1
                    spread[par, q4, 0, m, q4, 1, b, par, 1, m, b] = 1
    spread = spread.reshape(2, 128, 2048)

    pick = np.zeros((288, 1280), np.float32)
    for ri in range(2):
        for c in range(144):
            for q4 in range(4):
                pick[ri * 144 + c, ri * 640 + c // 18 * 80 + q4 * 20 + c % 18] = 1
    mask = np.zeros((2, 2, 4, 18, 8, 4, 20), np.float32)
    for par in range(2):
        for q4 in range(4):
            mask[par, par, q4, :, :, q4, :] = 1
    mask = mask.reshape(2, 144, 640)

    order = np.zeros((4, 2, 2, 16, 2, 2, 2, 2, 16, 8), np.float32)
    for xx in range(4):
        for par in range(2):
            for m in range(16):
                for b in range(2):
                    order[xx, par, 0, m, b, par, 0, 0, m, xx * 2 + b] = 1
                    order[xx, par, 1, m, b, par, 0, 1, m, xx * 2 + b] = 1
                    order[xx, par, 1, m, b, par, 1, 0, m, xx * 2 + b] = -1
                    order[xx, par, 0, m, b, par, 1, 1, m, xx * 2 + b] = 1
    order = order.reshape(512, 1024)

    bands = np.zeros((128, 4, 2, 2, 32), np.float32)
    for xx in range(4):
        for b in range(2):
            bands[xx * 2 + b, xx, :, b, :] = 1
    bands = bands.reshape(128, 512)

    q = np.arange(64)
    first = np.zeros((64, 128), np.float32)
    first[q, q // 4 % 8 * 8 + q // 32 * 4 + q % 4] = 1
    second = np.zeros((64, 64), np.float32)
    second[q, q // 2 % 8 * 8 + q % 2 * 4 + q // 16] = 1

    modes = np.zeros((144, 24), np.float32)
    modes[np.arange(144), np.arange(144) % 18] = 1
    half = lambda a: jnp.asarray(a, BF)
    small = [half(lattice), jnp.asarray(shift), half(bands), half(first), half(second), half(modes)]
    return small, [half(spread), half(pick), half(mask), half(order)]


def kernel(
    nz, ws_ref, wc_ref, g_ref, rot_ref, qp_ref, rotq_ref, freq_ref, modes_ref,
    lattice_ref, shift_ref, bands_ref, first_ref, second_ref, rowmode_ref, spread_in, pick_in, mask_in, order_in, o_ref,
    spread_ref, pick_ref, mask_ref, order_ref,
    gf, gl, kw, tf, kf, ksend, krecv, kx, ka, kbuf, ph, xf, win, wq, qbuf, bsend, brecv, mrecv, frecv, lhs, scale, rhs,
    of, osend, c_sem,
    ks_sem, kr_sem, ps_sem, pr_sem, ns_sem, nr_sem, ms_sem, mr_sem, fs_sem, fr_sem, zs_sem, zr_sem, bs_sem, br_sem,
    os_sem, or_sem,
):
    me = lax.axis_index("mode")
    pb = lax.axis_index("pb")
    x, z = pb // nz, pb % nz
    nr = nz * 16

    def at(xx, mm):
        return {"mode": mm, "pb": xx * nz + z}

    def remote(src, dst, ssem, rsem, where):
        return pltpu.make_async_remote_copy(
            src_ref=src, dst_ref=dst, send_sem=ssem, recv_sem=rsem,
            device_id=where, device_id_type=pl.DeviceIdType.MESH,
        )

    right = {"mode": me, "pb": x * nz + (z + 1) % nz}
    left = {"mode": me, "pb": x * nz + (z + nz - 1) % nz}

    barrier = pltpu.get_barrier_semaphore()

    @pl.loop(1, 32)
    def _(d):
        pl.semaphore_signal(
            barrier, inc=1, device_id=at((x + d // 8) % 4, (me + d) % 8), device_id_type=pl.DeviceIdType.MESH
        )

    if nz > 1:
        pl.semaphore_signal(barrier, inc=1, device_id=left, device_id_type=pl.DeviceIdType.MESH)
        pl.semaphore_signal(barrier, inc=1, device_id=right, device_id_type=pl.DeviceIdType.MESH)

    constant = [
        pltpu.make_async_copy(source, held, c_sem.at[n])
        for n, (source, held) in enumerate(
            ((spread_in, spread_ref), (pick_in, pick_ref), (mask_in, mask_ref), (order_in, order_ref))
        )
    ]
    for copy in constant:
        copy.start()

    lane = lax.broadcasted_iota(jnp.int32, (32, 512), 1)
    lane_i = lane % 32
    real = dot(rot_ref[0], bands_ref[...])
    imag = dot(rot_ref[1], bands_ref[...])
    in_real = lane % 128 < 64
    parts = (jnp.where(in_real, real, imag).astype(BF), jnp.where(in_real, -imag, real).astype(BF))
    for ri in range(2):
        part = parts[ri]

        @pl.loop(0, 32)
        def _(i):
            kw[pl.ds(pl.multiple_of(ri * 1024 + i * 32, 32), 32), :] = jnp.where(lane_i == i, part, 0.0).astype(BF)

    gf[...] = g_ref[...].astype(F32)
    for ri in range(2):
        for k in range(8):
            block = (ri * 8 + k) * 128
            gl[0:72, block:block + 128] = gf[pl.ds(k * 2 + ri, 72, stride=16), :].astype(BF)
    tf[...] = dot(gl[...], kw[...])
    kf[...] = jnp.zeros_like(kf)
    for xx in range(4):
        for r in range(4):
            kf[xx, pl.ds(r, 18, stride=4), :] = tf[r * 18:r * 18 + 18, xx * 128:(xx + 1) * 128]
    ksend[...] = kf[...].astype(BF)

    pl.semaphore_wait(barrier, 31 + (2 if nz > 1 else 0))

    for d in range(1, 4):
        xx = (x + d) % 4
        remote(ksend.at[xx], krecv.at[x], ks_sem.at[xx], kr_sem.at[x], at(xx, me)).start()
    krecv[x] = ksend[x]

    def rows_of(mm):
        return modes_ref.at[pl.ds(pl.multiple_of(mm * 144, 144), 144)]

    for d in range(1, 8):
        mm = (me + d) % 8
        remote(rows_of(mm), mrecv.at[me], ms_sem.at[mm], mr_sem.at[me], at(x, mm)).start()
        remote(freq_ref, frecv.at[me], fs_sem.at[mm], fr_sem.at[me], at(x, mm)).start()
    own_modes = pltpu.make_async_copy(rows_of(me), mrecv.at[me], c_sem.at[4])
    own_modes.start()
    frecv[me] = freq_ref[...]

    points = dot_t(first_ref[...], qp_ref[...]).astype(BF)
    inner = dot(points, lattice_ref[...]).astype(jnp.int32) & 31
    angle = inner.astype(F32) * (TWO_PI / 32)
    ph[x, 0:64, :] = jnp.cos(angle).astype(BF)
    ph[x, 64:128, :] = jnp.sin(angle).astype(BF)

    for d in range(1, 4):
        xx = (x + d) % 4
        remote(ksend.at[xx], krecv.at[xx], ks_sem.at[xx], kr_sem.at[xx], at(xx, me)).wait_recv()
    kx[...] = krecv[...].astype(F32)
    for xx in range(4):
        for r in range(4):
            ka[pl.ds(xx * 4 + r, 18, stride=16), :] = kx[xx, pl.ds(r, 18, stride=4), :]
    kbuf[z] = ka[...].astype(BF)

    def hop(way, step, part):
        shard = (z + (nz - step if way == 0 else step)) % nz
        piece = kbuf.at[shard, pl.ds(part * (288 // PARTS), 288 // PARTS)]
        return remote(piece, piece, zs_sem.at[way, step, part], zr_sem.at[way, step, part], right if way == 0 else left)

    hops = (nz // 2, nz - 1 - nz // 2)

    def advance(step):
        for part in range(PARTS):
            for way in range(2):
                if step < hops[way]:
                    if step > 0:
                        hop(way, step - 1, part).wait_recv()
                    hop(way, step, part).start()

    advance(0)
    for d in range(1, 4):
        xx = (x + d) % 4
        remote(ph.at[x], ph.at[x], ps_sem.at[xx], pr_sem.at[x], at(xx, me)).start()

    @pl.loop(0, 32)
    def _(i):
        both = [rotq_ref[pl.ds(pl.multiple_of(ri * 1024 + i * 32, 32), 32), :] for ri in range(2)]
        flipped = dot_t(second_ref[...], jnp.concatenate(both, axis=0))
        for q4 in range(4):
            xf[q4, pl.ds(i, 16, stride=32), :] = flipped[q4 * 16:(q4 + 1) * 16]

    lane_m = lax.broadcasted_iota(jnp.int32, (256, 128), 1) % 16
    for t in range(8):
        chosen = jnp.where((shift_ref[...] == ws_ref[t]) & (lane_m < wc_ref[t]), 1.0, 0.0).astype(BF)
        cut = jnp.zeros((64, 128), F32)
        for q4 in range(4):
            cut = cut + dot(xf[q4, t * 64:(t + 1) * 64, :].astype(BF), chosen[q4 * 64:(q4 + 1) * 64])
        win[x, 0, t * 32:(t + 1) * 32, :] = cut[0:32].astype(BF)
        win[x, 1, t * 32:(t + 1) * 32, :] = cut[32:64].astype(BF)
    for d in range(1, 4):
        xx = (x + d) % 4
        remote(win.at[x], win.at[x], ns_sem.at[xx], nr_sem.at[x], at(xx, me)).start()

    def weights(xx):
        for par in range(2):
            for q4 in range(4):
                spreaded = dot(win[xx, par], spread_ref[par, :, q4 * 512:(q4 + 1) * 512]).astype(BF)
                for g in range(4):
                    rows = spreaded[:, g * 128:(g + 1) * 128].reshape(8, 32, 128)
                    start = par * 128 + g * 32
                    wq[pl.ds(xx * 8, 8), q4, start:start + 32, :] = rows

    row_q = sum((lax.broadcasted_iota(jnp.int32, (144, 128), 0) >= 18 * n).astype(jnp.int32) for n in range(1, 8))
    diagonal = lax.broadcasted_iota(jnp.int32, (144, 128), 1) == row_q + me * 8

    def vectors(mm):
        own = 1.0 / jnp.sqrt(2.0 * frecv[mm])
        high = own.astype(BF)
        rest = own - high.astype(F32)
        middle = rest.astype(BF)
        low = (rest - middle.astype(F32)).astype(BF)
        by_row = dot(rowmode_ref[...], high) + dot(rowmode_ref[...], middle) + dot(rowmode_ref[...], low)
        scale[mm] = jnp.sum(jnp.where(diagonal, by_row, 0.0), axis=1, keepdims=True)
        both = dot(mrecv[mm], pick_ref[...]).astype(BF)
        for par in range(2):
            for ri in range(2):
                start = (par * 2 + ri) * 640
                lhs[mm, :, start:start + 640] = both[:, ri * 640:(ri + 1) * 640] * mask_ref[par]

    def wait_window(xx):
        remote(win.at[xx], win.at[xx], ns_sem.at[xx], nr_sem.at[xx], at(xx, me)).wait_recv()

    def wait_vectors(mm):
        remote(rows_of(mm), mrecv.at[mm], ms_sem.at[mm], mr_sem.at[mm], at(x, mm)).wait_recv()
        remote(freq_ref, frecv.at[mm], fs_sem.at[mm], fr_sem.at[mm], at(x, mm)).wait_recv()

    for step in range(8):
        if step > 0:
            advance(step)
        else:
            constant[0].wait()
            constant[1].wait()
            constant[2].wait()
            own_modes.wait()
        if step < 4:
            xx = (x + step) % 4
            if step > 0:
                wait_window(xx)
            weights(xx)
        mm = (me + step) % 8
        if step > 0:
            wait_vectors(mm)
        vectors(mm)
    for way in range(2):
        if hops[way]:
            for part in range(PARTS):
                hop(way, hops[way] - 1, part).wait_recv()

    for d in range(1, 4):
        xx = (x + d) % 4
        remote(ph.at[xx], ph.at[xx], ps_sem.at[xx], pr_sem.at[xx], at(xx, me)).wait_recv()
    qbuf[...] = jnp.zeros_like(qbuf)
    turn = lax.broadcasted_iota(jnp.int32, (64, 128), 1) < 64

    @pl.loop(0, 9)
    def _(cp):
        pair = [
            kbuf[:, pl.ds(pl.multiple_of((cp * 2 + p) * 16, 16), 16), :].reshape(nr, 128) for p in range(2)
        ]
        both = dot(ph[...].reshape(512, nr), jnp.concatenate(pair, axis=1))
        for p in range(2):
            for xx in range(4):
                along = both[xx * 128:xx * 128 + 64, p * 128:(p + 1) * 128]
                across = pltpu.roll(both[xx * 128 + 64:xx * 128 + 128, p * 128:(p + 1) * 128], 64, 1)
                total = along + jnp.where(turn, -across, across)
                for par in range(2):
                    qbuf[par, pl.ds(xx * 640 + cp * 2 + p, 32, stride=20), :] = total[par * 32:(par + 1) * 32]

    row = lax.broadcasted_iota(jnp.int32, (80, 256), 0)

    def band(xx, mm):
        spot = xx * 8 + mm
        rows = pl.ds(pl.multiple_of(spot * 80, 80), 80)
        own = jnp.concatenate([qbuf[0, rows, :], qbuf[1, rows, :]], axis=1)
        wide = [
            jnp.where((row >= q4 * 20) & (row < q4 * 20 + 20), own, 0.0).astype(BF) for q4 in range(4)
        ]
        return dot(jnp.concatenate(wide, axis=1), wq[spot].reshape(1024, 128)).astype(BF)

    def block(xx, mm, sx, sm):
        return remote(
            bsend.at[xx * 8 + mm], brecv.at[sx, sm], bs_sem.at[xx * 8 + mm], br_sem.at[sx * 8 + sm], at(xx, mm)
        )

    @pl.loop(1, 32)
    def _(d):
        xx, mm = (x + d // 8) % 4, (me + d) % 8
        bsend[xx * 8 + mm] = band(xx, mm)
        block(xx, mm, x, me).start()

    brecv[x, me] = band(x, me)

    @pl.loop(1, 32)
    def _(d):
        xx, mm = (x + d // 8) % 4, (me + d) % 8
        block(xx, mm, xx, mm).wait_recv()

    constant[3].wait()
    blocks = jnp.concatenate([brecv[xx].reshape(640, 128) for xx in range(4)], axis=1)
    for part in range(4):
        rhs[part * 640:(part + 1) * 640, :] = dot(blocks, order_ref[:, part * 256:(part + 1) * 256]).astype(BF)

    def finish(mm):
        done = dot(lhs[mm], rhs[...]) * scale[mm]
        for ri in range(2):
            of[pl.ds(ri, 144, stride=2), :] = done[:, ri * 128:(ri + 1) * 128]
        return of[...].astype(BF)

    @pl.loop(1, 8)
    def _(d):
        mm = (me + d) % 8
        osend[mm] = finish(mm)
        remote(osend.at[mm], o_ref.at[me], os_sem.at[mm], or_sem.at[me], at(x, mm)).start()

    o_ref[me] = finish(me)

    @pl.loop(1, 8)
    def _(d):
        mm = (me + d) % 8
        remote(osend.at[mm], o_ref.at[mm], os_sem.at[mm], or_sem.at[mm], at(x, mm)).wait()

    for d in range(1, 4):
        xx = (x + d) % 4
        remote(ksend.at[xx], krecv.at[x], ks_sem.at[xx], kr_sem.at[x], at(xx, me)).wait_send()
        remote(ph.at[x], ph.at[x], ps_sem.at[xx], pr_sem.at[x], at(xx, me)).wait_send()
        remote(win.at[x], win.at[x], ns_sem.at[xx], nr_sem.at[x], at(xx, me)).wait_send()
    for d in range(1, 8):
        mm = (me + d) % 8
        remote(rows_of(mm), mrecv.at[me], ms_sem.at[mm], mr_sem.at[me], at(x, mm)).wait_send()
        remote(freq_ref, frecv.at[me], fs_sem.at[mm], fr_sem.at[me], at(x, mm)).wait_send()
    for way in range(2):
        for step in range(hops[way]):
            for part in range(PARTS):
                hop(way, step, part).wait_send()

    @pl.loop(1, 32)
    def _(d):
        xx, mm = (x + d // 8) % 4, (me + d) % 8
        block(xx, mm, x, me).wait_send()


def shards(g_wann, rot_k, qpoints, rot_kq, win_count, win_start, modes_vec, frequencies):
    nz = lax.axis_size("pb") // NX
    small, large = constants(nz)

    g_rows = g_wann.reshape(4, 2, 18, 8, 128).transpose(0, 2, 3, 1, 4).reshape(1152, 128)
    rot = jnp.pad(rot_k, ((0, 0), (0, 0), (0, 120)))
    points = jnp.pad(qpoints.astype(BF), ((0, 125), (0, 64)))
    rotq = rot_kq.transpose(1, 2, 3, 0).reshape(2048, 64)
    freq = jnp.pad(frequencies.T, ((0, 6), (0, 64)), constant_values=1.0)
    modes = modes_vec.transpose(0, 2, 1, 3).reshape(1152, 288)

    vmem = pl.BlockSpec(memory_space=pltpu.VMEM)
    smem = pl.BlockSpec(memory_space=pltpu.SMEM)
    whole = pl.BlockSpec(memory_space=pl.ANY)
    sem = pltpu.SemaphoreType.DMA
    out = pl.pallas_call(
        functools.partial(kernel, nz),
        out_shape=jax.ShapeDtypeStruct((8, 288, 128), BF),
        in_specs=[smem, smem] + [vmem] * 12 + [whole] * 4,
        out_specs=vmem,
        scratch_shapes=[
            pltpu.VMEM((2, 128, 2048), BF),
            pltpu.VMEM((288, 1280), BF),
            pltpu.VMEM((2, 144, 640), BF),
            pltpu.VMEM((512, 1024), BF),
            pltpu.VMEM((1152, 128), F32),
            pltpu.VMEM((80, 2048), BF),
            pltpu.VMEM((2048, 512), BF),
            pltpu.VMEM((80, 512), F32),
            pltpu.VMEM((4, 80, 128), F32),
            pltpu.VMEM((4, 80, 128), BF),
            pltpu.VMEM((4, 80, 128), BF),
            pltpu.VMEM((4, 80, 128), F32),
            pltpu.VMEM((288, 128), F32),
            pltpu.VMEM((nz, 288, 128), BF),
            pltpu.VMEM((4, 128, nz * 16), BF),
            pltpu.VMEM((4, 512, 64), F32),
            pltpu.VMEM((4, 2, 256, 128), BF),
            pltpu.VMEM((32, 4, 256, 128), BF),
            pltpu.VMEM((2, 2560, 128), F32),
            pltpu.VMEM((32, 80, 128), BF),
            pltpu.VMEM((4, 8, 80, 128), BF),
            pltpu.VMEM((8, 144, 288), BF),
            pltpu.VMEM((8, 24, 128), F32),
            pltpu.VMEM((8, 144, 2560), BF),
            pltpu.VMEM((8, 144, 1), F32),
            pltpu.VMEM((2560, 256), BF),
            pltpu.VMEM((288, 128), F32),
            pltpu.VMEM((8, 288, 128), BF),
            sem((5,)),
            sem((4,)), sem((4,)), sem((4,)), sem((4,)), sem((4,)), sem((4,)), sem((8,)), sem((8,)), sem((8,)), sem((8,)),
            sem((2, 8, PARTS)), sem((2, 8, PARTS)), sem((32,)), sem((32,)), sem((8,)), sem((8,)),
        ],
        compiler_params=pltpu.CompilerParams(
            collective_id=0, has_side_effects=True, vmem_limit_bytes=56 * 1024 * 1024
        ),
    )(win_start, win_count, g_rows, rot, points, rotq, freq, modes, *small, *large)
    return out.reshape(64, 18, 2, 128).transpose(0, 2, 1, 3)


def solution(mesh):
    placed = (
        P("pb", None, "mode", None),
        P(),
        P(None, "pb"),
        P("pb", None, None, None),
        P("pb"),
        P("pb"),
        P("pb", None, "mode", None),
        P("pb", "mode"),
    )
    return jax.shard_map(
        shards, mesh=mesh, in_specs=placed, out_specs=P("pb", None, "mode", None), check_vma=False
    )
```

```python
import functools
import jax
import jax.numpy as jnp
import numpy as np
from jax import lax
from jax.experimental import pallas as pl
from jax.experimental.pallas import tpu as pltpu
from jax.sharding import PartitionSpec as P

NX = 4
NM = 8
TWO_PI = 6.283185307179586
BF = jnp.bfloat16
F32 = jnp.float32


def dot(a, b):
    return jnp.dot(a, b, preferred_element_type=F32)


def dot_t(a, b):
    return lax.dot_general(a, b, (((1,), (1,)), ((), ())), preferred_element_type=F32)


def constants(nz):
    rows = np.arange(nz * 16)
    z, x, r4 = rows // 16, rows // 4 % 4, rows % 4
    r = (x * nz + z) * 4 + r4
    lattice = np.zeros((8, nz * 16), np.float32)
    lattice[0] = r % 8 - 4
    lattice[1] = r // 8 % 8 - 4
    lattice[2] = r // 64 - 4

    row, lane = np.arange(256)[:, None], np.arange(128)[None, :]
    same = row // 32 == lane // 16
    shift = np.where(same, row % 32 - lane % 16, -1000).astype(np.int32)

    spread = np.zeros((2, 4, 2, 16, 4, 2, 2, 2, 2, 16, 2), np.float32)
    for par in range(2):
        for q4 in range(4):
            for m in range(16):
                for b in range(2):
                    spread[par, q4, 0, m, q4, 0, b, par, 0, m, b] = 1
                    spread[par, q4, 1, m, q4, 1, b, par, 0, m, b] = 1
                    spread[par, q4, 1, m, q4, 0, b, par, 1, m, b] = -1
                    spread[par, q4, 0, m, q4, 1, b, par, 1, m, b] = 1
    spread = spread.reshape(2, 128, 2048)

    pick = np.zeros((288, 1280), np.float32)
    for ri in range(2):
        for c in range(144):
            for q4 in range(4):
                pick[ri * 144 + c, ri * 640 + c // 18 * 80 + q4 * 20 + c % 18] = 1
    mask = np.zeros((2, 2, 4, 18, 8, 4, 20), np.float32)
    for par in range(2):
        for q4 in range(4):
            mask[par, par, q4, :, :, q4, :] = 1
    mask = mask.reshape(2, 144, 640)

    order = np.zeros((4, 2, 2, 16, 2, 2, 2, 2, 16, 8), np.float32)
    for xx in range(4):
        for par in range(2):
            for m in range(16):
                for b in range(2):
                    order[xx, par, 0, m, b, par, 0, 0, m, xx * 2 + b] = 1
                    order[xx, par, 1, m, b, par, 0, 1, m, xx * 2 + b] = 1
                    order[xx, par, 1, m, b, par, 1, 0, m, xx * 2 + b] = -1
                    order[xx, par, 0, m, b, par, 1, 1, m, xx * 2 + b] = 1
    order = order.reshape(512, 1024)

    bands = np.zeros((8, 4, 2, 2, 32), np.float32)
    for xx in range(4):
        for b in range(2):
            bands[xx * 2 + b, xx, :, b, :] = 1
    bands = bands.reshape(8, 512)

    q = np.arange(64)
    first = np.zeros((64, 128), np.float32)
    first[q, q // 4 % 8 * 8 + q // 32 * 4 + q % 4] = 1
    second = np.zeros((64, 64), np.float32)
    second[q, q // 2 % 8 * 8 + q % 2 * 4 + q // 16] = 1

    modes = np.zeros((144, 24), np.float32)
    modes[np.arange(144), np.arange(144) % 18] = 1
    half = lambda a: jnp.asarray(a, BF)
    small = [half(lattice), jnp.asarray(shift), half(bands), half(first), half(second), half(modes)]
    return small, [half(spread), half(pick), half(mask), half(order)]


def kernel(
    nz, ws_ref, wc_ref, g_ref, rot_ref, qp_ref, rotq_ref, freq_ref, modes_ref,
    lattice_ref, shift_ref, bands_ref, first_ref, second_ref, rowmode_ref, spread_in, pick_in, mask_in, order_in, o_ref,
    spread_ref, pick_ref, mask_ref, order_ref,
    gf, gl, kw, tf, qs, fs, kf, ksend, krecv, kx, ka, kbuf, ph, xf, win, wq, qbuf, bsend, brecv, mrecv, frecv, lhs, scale, rhs,
    of, osend, c_sem,
    ks_sem, kr_sem, ps_sem, pr_sem, ns_sem, nr_sem, ms_sem, mr_sem, fs_sem, fr_sem, zs_sem, zr_sem, bs_sem, br_sem,
    os_sem, or_sem,
):
    me = lax.axis_index("mode")
    pb = lax.axis_index("pb")
    x, z = pb // nz, pb % nz
    nr = nz * 16

    def at(xx, mm):
        return {"mode": mm, "pb": xx * nz + z}

    def remote(src, dst, ssem, rsem, where):
        return pltpu.make_async_remote_copy(
            src_ref=src, dst_ref=dst, send_sem=ssem, recv_sem=rsem,
            device_id=where, device_id_type=pl.DeviceIdType.MESH,
        )

    def along_z(step):
        return {"mode": me, "pb": x * nz + (z + nz + step) % nz}

    barrier = pltpu.get_barrier_semaphore()

    @pl.loop(1, 32)
    def _(d):
        pl.semaphore_signal(
            barrier, inc=1, device_id=at((x + d // 8) % 4, (me + d) % 8), device_id_type=pl.DeviceIdType.MESH
        )

    near = (-3, 3, -1, 1, -2, 2)
    for step in near:
        pl.semaphore_signal(barrier, inc=1, device_id=along_z(step), device_id_type=pl.DeviceIdType.MESH)

    constant = [
        pltpu.make_async_copy(source, held, c_sem.at[n])
        for n, (source, held) in enumerate(
            ((spread_in, spread_ref), (pick_in, pick_ref), (mask_in, mask_ref), (order_in, order_ref))
        )
    ]
    for copy in constant:
        copy.start()

    lane = lax.broadcasted_iota(jnp.int32, (32, 512), 1)
    lane_i = lane % 32
    turn_b = lambda ri: lax.dot_general(
        rot_ref[ri], bands_ref[...], (((0,), (0,)), ((), ())), preferred_element_type=F32
    )
    real, imag = turn_b(0), turn_b(1)
    in_real = lane % 128 < 64
    parts = (jnp.where(in_real, real, imag).astype(BF), jnp.where(in_real, -imag, real).astype(BF))
    for ri in range(2):
        part = parts[ri]

        @pl.loop(0, 32)
        def _(i):
            kw[pl.ds(pl.multiple_of(ri * 1024 + i * 32, 32), 32), :] = jnp.where(lane_i == i, part, 0.0).astype(BF)

    gf[...] = g_ref[...].astype(F32)
    for ri in range(2):
        for k in range(8):
            block = (ri * 8 + k) * 128
            gl[0:72, block:block + 128] = gf[pl.ds(k * 2 + ri, 72, stride=16), :].astype(BF)
    tf[...] = dot(gl[...], kw[...])
    kf[...] = jnp.zeros_like(kf)
    for xx in range(4):
        for r in range(4):
            kf[xx, pl.ds(r, 18, stride=4), :] = tf[r * 18:r * 18 + 18, xx * 128:(xx + 1) * 128]
    ksend[...] = kf[...].astype(BF)

    pl.semaphore_wait(barrier, 31 + len(near))

    for d in range(1, 4):
        xx = (x + d) % 4
        remote(ksend.at[xx], krecv.at[x], ks_sem.at[xx], kr_sem.at[x], at(xx, me)).start()
    krecv[x] = ksend[x]

    def rows_of(mm):
        return modes_ref.at[pl.ds(pl.multiple_of(mm * 144, 144), 144)]

    fs[...] = jnp.ones_like(fs)
    fs[0:18, 0:64] = freq_ref[...]
    for d in range(1, 8):
        mm = (me + d) % 8
        remote(rows_of(mm), mrecv.at[me], ms_sem.at[mm], mr_sem.at[me], at(x, mm)).start()
        remote(fs, frecv.at[me], fs_sem.at[mm], fr_sem.at[me], at(x, mm)).start()
    own_modes = pltpu.make_async_copy(rows_of(me), mrecv.at[me], c_sem.at[4])
    own_modes.start()
    frecv[me] = fs[...]

    qs[...] = jnp.zeros_like(qs)
    qs[0:3, 0:64] = qp_ref[...].astype(F32)
    points = dot_t(first_ref[...], qs[...].astype(BF)).astype(BF)
    inner = dot(points, lattice_ref[...]).astype(jnp.int32) & 31
    angle = inner.astype(F32) * (TWO_PI / 32)
    ph[x, 0:64, :] = jnp.cos(angle).astype(BF)
    ph[x, 64:128, :] = jnp.sin(angle).astype(BF)

    for d in range(1, 4):
        xx = (x + d) % 4
        remote(ksend.at[xx], krecv.at[xx], ks_sem.at[xx], kr_sem.at[xx], at(xx, me)).wait_recv()
    kx[...] = krecv[...].astype(F32)
    for xx in range(4):
        for r in range(4):
            ka[pl.ds(xx * 4 + r, 18, stride=16), :] = kx[xx, pl.ds(r, 18, stride=4), :]
    kbuf[z] = ka[...].astype(BF)

    def hop(offset, step, part):
        spot = (offset - step) % nz
        piece = kbuf.at[(z + nz + offset) % nz, pl.ds(part * 144, 144)]
        return remote(piece, piece, zs_sem.at[spot, part], zr_sem.at[spot, part], along_z(step))

    def came(offset, part):
        hop(offset, 0, part).wait_recv()

    routes = {0: (3, -3, 1, -1), -3: (3, 1, -1), 3: (-3, 1, -1), -6: (1, -1), 6: (1, -1)}

    def pass_on(first, second):
        for part in range(2):
            for offset in (first, second):
                came(offset, part)
                for step in routes[offset]:
                    hop(offset, step, part).start()
                if (offset, part) in ((-6, 0), (6, 1)):
                    hop(offset, 2 if part == 0 else -2, part).start()

    for part in range(2):
        for step in routes[0]:
            hop(0, step, part).start()
    for d in range(1, 4):
        xx = (x + d) % 4
        remote(ph.at[x], ph.at[x], ps_sem.at[xx], pr_sem.at[x], at(xx, me)).start()

    @pl.loop(0, 32)
    def _(i):
        both = [rotq_ref[pl.ds(pl.multiple_of(ri * 1024 + i * 32, 32), 32), :] for ri in range(2)]
        flipped = dot_t(second_ref[...], jnp.concatenate(both, axis=0))
        for q4 in range(4):
            xf[q4, pl.ds(i, 16, stride=32), :] = flipped[q4 * 16:(q4 + 1) * 16]

    lane_m = lax.broadcasted_iota(jnp.int32, (256, 128), 1) % 16
    for t in range(8):
        chosen = jnp.where((shift_ref[...] == ws_ref[t]) & (lane_m < wc_ref[t]), 1.0, 0.0).astype(BF)
        cut = jnp.zeros((64, 128), F32)
        for q4 in range(4):
            cut = cut + dot(xf[q4, t * 64:(t + 1) * 64, :].astype(BF), chosen[q4 * 64:(q4 + 1) * 64])
        win[x, 0, t * 32:(t + 1) * 32, :] = cut[0:32].astype(BF)
        win[x, 1, t * 32:(t + 1) * 32, :] = cut[32:64].astype(BF)
    for d in range(1, 4):
        xx = (x + d) % 4
        remote(win.at[x], win.at[x], ns_sem.at[xx], nr_sem.at[x], at(xx, me)).start()

    def weights(xx):
        for par in range(2):
            for q4 in range(4):
                spreaded = dot(win[xx, par], spread_ref[par, :, q4 * 512:(q4 + 1) * 512]).astype(BF)
                for g in range(4):
                    rows = spreaded[:, g * 128:(g + 1) * 128].reshape(8, 32, 128)
                    start = par * 128 + g * 32
                    wq[pl.ds(xx * 8, 8), q4, start:start + 32, :] = rows

    row_q = sum((lax.broadcasted_iota(jnp.int32, (144, 128), 0) >= 18 * n).astype(jnp.int32) for n in range(1, 8))
    diagonal = lax.broadcasted_iota(jnp.int32, (144, 128), 1) == row_q + me * 8

    def vectors(mm):
        own = 1.0 / jnp.sqrt(2.0 * frecv[mm])
        high = own.astype(BF)
        rest = own - high.astype(F32)
        middle = rest.astype(BF)
        low = (rest - middle.astype(F32)).astype(BF)
        by_row = dot(rowmode_ref[...], high) + dot(rowmode_ref[...], middle) + dot(rowmode_ref[...], low)
        scale[mm] = jnp.sum(jnp.where(diagonal, by_row, 0.0), axis=1, keepdims=True)
        both = dot(mrecv[mm], pick_ref[...]).astype(BF)
        for par in range(2):
            for ri in range(2):
                start = (par * 2 + ri) * 640
                lhs[mm, :, start:start + 640] = both[:, ri * 640:(ri + 1) * 640] * mask_ref[par]

    def wait_window(xx):
        remote(win.at[xx], win.at[xx], ns_sem.at[xx], nr_sem.at[xx], at(xx, me)).wait_recv()

    def wait_vectors(mm):
        remote(rows_of(mm), mrecv.at[mm], ms_sem.at[mm], mr_sem.at[mm], at(x, mm)).wait_recv()
        remote(fs, frecv.at[mm], fs_sem.at[mm], fr_sem.at[mm], at(x, mm)).wait_recv()

    pass_on(-3, 3)
    for copy in constant[:3]:
        copy.wait()
    own_modes.wait()
    weights(x)
    vectors(me)
    pass_on(-6, 6)
    for d in range(1, 4):
        wait_window((x + d) % 4)
        weights((x + d) % 4)
    for d in range(1, 8):
        wait_vectors((me + d) % 8)
        vectors((me + d) % 8)
    for offset in (-1, 1, -4, 4, -7, 7, -2, 2, -5, 5, 8):
        for part in range(2):
            came(offset, part)

    for d in range(1, 4):
        xx = (x + d) % 4
        remote(ph.at[xx], ph.at[xx], ps_sem.at[xx], pr_sem.at[xx], at(xx, me)).wait_recv()
    qbuf[...] = jnp.zeros_like(qbuf)
    turn = lax.broadcasted_iota(jnp.int32, (64, 128), 1) < 64

    @pl.loop(0, 9)
    def _(cp):
        pair = [
            kbuf[:, pl.ds(pl.multiple_of((cp * 2 + p) * 16, 16), 16), :].reshape(nr, 128) for p in range(2)
        ]
        both = dot(ph[...].reshape(512, nr), jnp.concatenate(pair, axis=1))
        for p in range(2):
            for xx in range(4):
                along = both[xx * 128:xx * 128 + 64, p * 128:(p + 1) * 128]
                across = pltpu.roll(both[xx * 128 + 64:xx * 128 + 128, p * 128:(p + 1) * 128], 64, 1)
                total = along + jnp.where(turn, -across, across)
                for par in range(2):
                    qbuf[par, pl.ds(xx * 640 + cp * 2 + p, 32, stride=20), :] = total[par * 32:(par + 1) * 32]

    row = lax.broadcasted_iota(jnp.int32, (80, 256), 0)

    def band(xx, mm):
        spot = xx * 8 + mm
        rows = pl.ds(pl.multiple_of(spot * 80, 80), 80)
        own = jnp.concatenate([qbuf[0, rows, :], qbuf[1, rows, :]], axis=1)
        wide = [
            jnp.where((row >= q4 * 20) & (row < q4 * 20 + 20), own, 0.0).astype(BF) for q4 in range(4)
        ]
        return dot(jnp.concatenate(wide, axis=1), wq[spot].reshape(1024, 128)).astype(BF)

    def block(xx, mm, sx, sm):
        return remote(
            bsend.at[xx * 8 + mm], brecv.at[sx, sm], bs_sem.at[xx * 8 + mm], br_sem.at[sx * 8 + sm], at(xx, mm)
        )

    @pl.loop(1, 4)
    def _(d):
        xx = (x + d) % 4
        for half in range(2):
            for mm in range(half * 4, half * 4 + 4):
                bsend[xx * 8 + mm] = band(xx, mm)
            for mm in range(half * 4, half * 4 + 4):
                block(xx, mm, x, me).start()

    for d in range(1, 8):
        bsend[x * 8 + (me + d) % 8] = band(x, (me + d) % 8)
        block(x, (me + d) % 8, x, me).start()
    brecv[x, me] = band(x, me)

    @pl.loop(1, 32)
    def _(d):
        xx, mm = (x + d // 8) % 4, (me + d) % 8
        block(xx, mm, xx, mm).wait_recv()

    constant[3].wait()
    blocks = jnp.concatenate([brecv[xx].reshape(640, 128) for xx in range(4)], axis=1)
    for part in range(4):
        rhs[part * 640:(part + 1) * 640, :] = dot(blocks, order_ref[:, part * 256:(part + 1) * 256]).astype(BF)

    def finish(chip):
        done = dot(lhs[pl.ds(chip * 2, 2)].reshape(288, 2560), rhs[...])
        for n in range(2):
            one = done[n * 144:(n + 1) * 144] * scale[chip * 2 + n]
            for ri in range(2):
                of[n, pl.ds(ri, 144, stride=2), :] = one[:, ri * 128:(ri + 1) * 128]
            osend[chip * 2 + n] = of[n].astype(BF)

    def send_out(mm):
        remote(osend.at[mm], o_ref.at[me], os_sem.at[mm], or_sem.at[me], at(x, mm)).start()

    for d in (2, 1, 3):
        chip = (me // 2 + d) % 4
        finish(chip)
        send_out(chip * 2 + me % 2)
        send_out(chip * 2 + 1 - me % 2)
    finish(me // 2)
    send_out(me // 2 * 2 + 1 - me % 2)
    o_ref[me] = osend[me]

    @pl.loop(1, 8)
    def _(d):
        mm = (me + d) % 8
        remote(osend.at[mm], o_ref.at[mm], os_sem.at[mm], or_sem.at[mm], at(x, mm)).wait()

    for d in range(1, 4):
        xx = (x + d) % 4
        remote(ksend.at[xx], krecv.at[x], ks_sem.at[xx], kr_sem.at[x], at(xx, me)).wait_send()
        remote(ph.at[x], ph.at[x], ps_sem.at[xx], pr_sem.at[x], at(xx, me)).wait_send()
        remote(win.at[x], win.at[x], ns_sem.at[xx], nr_sem.at[x], at(xx, me)).wait_send()
    for d in range(1, 8):
        mm = (me + d) % 8
        remote(rows_of(mm), mrecv.at[me], ms_sem.at[mm], mr_sem.at[me], at(x, mm)).wait_send()
        remote(fs, frecv.at[me], fs_sem.at[mm], fr_sem.at[me], at(x, mm)).wait_send()
    for part in range(2):
        for offset, steps in routes.items():
            for step in steps:
                hop(offset, step, part).wait_send()
    hop(-6, 2, 0).wait_send()
    hop(6, -2, 1).wait_send()

    @pl.loop(1, 32)
    def _(d):
        xx, mm = (x + d // 8) % 4, (me + d) % 8
        block(xx, mm, x, me).wait_send()


def shards(g_wann, rot_k, qpoints, rot_kq, win_count, win_start, modes_vec, frequencies):
    nz = lax.axis_size("pb") // NX
    small, large = constants(nz)

    g_rows = g_wann.reshape(4, 2, 18, 8, 128).transpose(0, 2, 3, 1, 4).reshape(1152, 128)
    rot = rot_k.transpose(0, 2, 1)
    rotq = rot_kq.transpose(1, 2, 3, 0).reshape(2048, 64)
    freq = frequencies.T
    modes = modes_vec.transpose(0, 2, 1, 3).reshape(1152, 288)

    vmem = pl.BlockSpec(memory_space=pltpu.VMEM)
    smem = pl.BlockSpec(memory_space=pltpu.SMEM)
    whole = pl.BlockSpec(memory_space=pl.ANY)
    sem = pltpu.SemaphoreType.DMA
    out = pl.pallas_call(
        functools.partial(kernel, nz),
        out_shape=jax.ShapeDtypeStruct((8, 288, 128), BF),
        in_specs=[smem, smem] + [vmem] * 12 + [whole] * 4,
        out_specs=vmem,
        scratch_shapes=[
            pltpu.VMEM((2, 128, 2048), BF),
            pltpu.VMEM((288, 1280), BF),
            pltpu.VMEM((2, 144, 640), BF),
            pltpu.VMEM((512, 1024), BF),
            pltpu.VMEM((1152, 128), F32),
            pltpu.VMEM((80, 2048), BF),
            pltpu.VMEM((2048, 512), BF),
            pltpu.VMEM((80, 512), F32),
            pltpu.VMEM((8, 128), F32),
            pltpu.VMEM((24, 128), F32),
            pltpu.VMEM((4, 80, 128), F32),
            pltpu.VMEM((4, 80, 128), BF),
            pltpu.VMEM((4, 80, 128), BF),
            pltpu.VMEM((4, 80, 128), F32),
            pltpu.VMEM((288, 128), F32),
            pltpu.VMEM((nz, 288, 128), BF),
            pltpu.VMEM((4, 128, nz * 16), BF),
            pltpu.VMEM((4, 512, 64), F32),
            pltpu.VMEM((4, 2, 256, 128), BF),
            pltpu.VMEM((32, 4, 256, 128), BF),
            pltpu.VMEM((2, 2560, 128), F32),
            pltpu.VMEM((32, 80, 128), BF),
            pltpu.VMEM((4, 8, 80, 128), BF),
            pltpu.VMEM((8, 144, 288), BF),
            pltpu.VMEM((8, 24, 128), F32),
            pltpu.VMEM((8, 144, 2560), BF),
            pltpu.VMEM((8, 144, 1), F32),
            pltpu.VMEM((2560, 256), BF),
            pltpu.VMEM((2, 288, 128), F32),
            pltpu.VMEM((8, 288, 128), BF),
            sem((5,)),
            sem((4,)), sem((4,)), sem((4,)), sem((4,)), sem((4,)), sem((4,)), sem((8,)), sem((8,)), sem((8,)), sem((8,)),
            sem((16, 2)), sem((16, 2)), sem((32,)), sem((32,)), sem((8,)), sem((8,)),
        ],
        compiler_params=pltpu.CompilerParams(
            collective_id=0, has_side_effects=True, vmem_limit_bytes=56 * 1024 * 1024
        ),
    )(win_start, win_count, g_rows, rot, qpoints, rotq, freq, modes, *small, *large)
    return out.reshape(64, 18, 2, 128).transpose(0, 2, 1, 3)


def solution(mesh):
    placed = (
        P("pb", None, "mode", None),
        P(),
        P(None, "pb"),
        P("pb", None, None, None),
        P("pb"),
        P("pb"),
        P("pb", None, "mode", None),
        P("pb", "mode"),
    )
    return jax.shard_map(
        shards, mesh=mesh, in_specs=placed, out_specs=P("pb", None, "mode", None), check_vma=False
    )
```

```python
import functools
import jax
import jax.numpy as jnp
import numpy as np
from jax import lax
from jax.experimental import pallas as pl
from jax.experimental.pallas import tpu as pltpu
from jax.sharding import PartitionSpec as P

NX = 4
NM = 8
TWO_PI = 6.283185307179586
BF = jnp.bfloat16
F32 = jnp.float32


def dot(a, b):
    return jnp.dot(a, b, preferred_element_type=F32)


def dot_t(a, b):
    return lax.dot_general(a, b, (((1,), (1,)), ((), ())), preferred_element_type=F32)


def constants(nz):
    rows = np.arange(nz * 16)
    z, x, r4 = rows // 16, rows // 4 % 4, rows % 4
    r = (x * nz + z) * 4 + r4
    lattice = np.zeros((8, nz * 16), np.float32)
    lattice[0] = r % 8 - 4
    lattice[1] = r // 8 % 8 - 4
    lattice[2] = r // 64 - 4

    row, lane = np.arange(256)[:, None], np.arange(128)[None, :]
    same = row // 32 == lane // 16
    shift = np.where(same, row % 32 - lane % 16, -1000).astype(np.int32)

    spread = np.zeros((2, 4, 2, 16, 4, 2, 2, 2, 2, 16, 2), np.float32)
    for par in range(2):
        for q4 in range(4):
            for m in range(16):
                for b in range(2):
                    spread[par, q4, 0, m, q4, 0, b, par, 0, m, b] = 1
                    spread[par, q4, 1, m, q4, 1, b, par, 0, m, b] = 1
                    spread[par, q4, 1, m, q4, 0, b, par, 1, m, b] = -1
                    spread[par, q4, 0, m, q4, 1, b, par, 1, m, b] = 1
    spread = spread.reshape(2, 128, 2048)

    pick = np.zeros((256, 640), np.float32)
    for c in range(144):
        for q4 in range(4):
            pick[c, c // 18 * 80 + q4 * 20 + c % 18] = 1
    mask = np.zeros((2, 2, 4, 18, 8, 4, 20), np.float32)
    for par in range(2):
        for q4 in range(4):
            mask[par, par, q4, :, :, q4, :] = 1
    mask = mask.reshape(2, 144, 640)

    order = np.zeros((4, 2, 2, 16, 2, 2, 2, 2, 16, 8), np.float32)
    for xx in range(4):
        for par in range(2):
            for m in range(16):
                for b in range(2):
                    order[xx, par, 0, m, b, par, 0, 0, m, xx * 2 + b] = 1
                    order[xx, par, 1, m, b, par, 0, 1, m, xx * 2 + b] = 1
                    order[xx, par, 1, m, b, par, 1, 0, m, xx * 2 + b] = -1
                    order[xx, par, 0, m, b, par, 1, 1, m, xx * 2 + b] = 1
    order = order.reshape(512, 1024)

    bands = np.zeros((8, 4, 2, 2, 32), np.float32)
    for xx in range(4):
        for b in range(2):
            bands[xx * 2 + b, xx, :, b, :] = 1
    bands = bands.reshape(8, 512)

    q = np.arange(64)
    first = np.zeros((64, 128), np.float32)
    first[q, q // 4 % 8 * 8 + q // 32 * 4 + q % 4] = 1
    second = np.zeros((64, 64), np.float32)
    second[q, q // 2 % 8 * 8 + q % 2 * 4 + q // 16] = 1

    gather = np.zeros((18, 4, 4, 4, 80), np.float32)
    for c in range(18):
        for xx in range(4):
            for r4 in range(4):
                gather[c, xx, r4, xx, c * 4 + r4] = 1
    gather = gather.reshape(288, 320)

    modes = np.zeros((144, 24), np.float32)
    modes[np.arange(144), np.arange(144) % 18] = 1
    half = lambda a: jnp.asarray(a, BF)
    small = [half(lattice), jnp.asarray(shift), half(bands), half(first), half(second), half(modes), half(gather)]
    return small, [half(spread), half(pick), half(mask), half(order)]


def kernel(
    nz, ws_ref, wc_ref, g_ref, rot_ref, qp_ref, rotq_ref, freq_ref, modes_ref,
    lattice_ref, shift_ref, bands_ref, first_ref, second_ref, rowmode_ref, gather_ref, spread_in, pick_in, mask_in, order_in, o_ref,
    spread_ref, pick_ref, mask_ref, order_ref,
    gf, gl, kw, tf, qs, fs, kf, ksend, kraw, kbuf, ph, xf, win, wq, qbuf, bsend, brecv, mrecv, mf, frecv, lhs, scale, rhs,
    of, osend, c_sem,
    ks_sem, kr_sem, ps_sem, pr_sem, ns_sem, nr_sem, ms_sem, mr_sem, fs_sem, fr_sem, zs_sem, zr_sem, bs_sem, br_sem,
    os_sem, or_sem,
):
    me = lax.axis_index("mode")
    pb = lax.axis_index("pb")
    x, z = pb // nz, pb % nz
    nr = nz * 16

    def at(xx, mm):
        return {"mode": mm, "pb": xx * nz + z}

    def remote(src, dst, ssem, rsem, where):
        return pltpu.make_async_remote_copy(
            src_ref=src, dst_ref=dst, send_sem=ssem, recv_sem=rsem,
            device_id=where, device_id_type=pl.DeviceIdType.MESH,
        )

    def along_z(step, xx=None):
        return {"mode": me, "pb": (x if xx is None else xx) * nz + (z + nz + step) % nz}

    barrier = pltpu.get_barrier_semaphore()

    @pl.loop(1, 32)
    def _(d):
        pl.semaphore_signal(
            barrier, inc=1, device_id=at((x + d // 8) % 4, (me + d) % 8), device_id_type=pl.DeviceIdType.MESH
        )

    near = (3, -3, 1, -1)
    for step in near:
        for xx in range(4):
            pl.semaphore_signal(barrier, inc=1, device_id=along_z(step, xx), device_id_type=pl.DeviceIdType.MESH)
    for step in (2, -2):
        pl.semaphore_signal(barrier, inc=1, device_id=along_z(step), device_id_type=pl.DeviceIdType.MESH)

    qbuf[...] = jnp.zeros_like(qbuf)
    mf[...] = jnp.zeros_like(mf)
    constant = [
        pltpu.make_async_copy(source, held, c_sem.at[n])
        for n, (source, held) in enumerate(
            ((spread_in, spread_ref), (pick_in, pick_ref), (mask_in, mask_ref), (order_in, order_ref))
        )
    ]
    for copy in constant:
        copy.start()

    lane = lax.broadcasted_iota(jnp.int32, (32, 512), 1)
    lane_i = lane % 32
    turn_b = lambda ri: lax.dot_general(
        rot_ref[ri], bands_ref[...], (((0,), (0,)), ((), ())), preferred_element_type=F32
    )
    real, imag = turn_b(0), turn_b(1)
    in_real = lane % 128 < 64
    parts = (jnp.where(in_real, real, imag).astype(BF), jnp.where(in_real, -imag, real).astype(BF))
    for ri in range(2):
        part = parts[ri]

        @pl.loop(0, 32)
        def _(i):
            kw[pl.ds(pl.multiple_of(ri * 1024 + i * 32, 32), 32), :] = jnp.where(lane_i == i, part, 0.0).astype(BF)

    gf[...] = g_ref[...].astype(F32)
    for ri in range(2):
        for k in range(8):
            block = (ri * 8 + k) * 128
            gl[0:72, block:block + 128] = gf[pl.ds(k * 2 + ri, 72, stride=16), :].astype(BF)
    tf[...] = dot(gl[...], kw[...])
    kf[...] = jnp.zeros_like(kf)
    for xx in range(4):
        for r in range(4):
            kf[xx, pl.ds(r, 18, stride=4), :] = tf[r * 18:r * 18 + 18, xx * 128:(xx + 1) * 128]
    ksend[...] = kf[...].astype(BF)

    pl.semaphore_wait(barrier, 31 + 4 * len(near) + 2)

    def first(slot, step, xx):
        return remote(ksend.at[xx], kraw.at[z, x], ks_sem.at[slot, xx], kr_sem.at[slot, x], along_z(step, xx))

    def first_came(slot, step, xx):
        home = kraw.at[(z + nz - step) % nz, xx]
        remote(ksend.at[xx], home, ks_sem.at[slot, xx], kr_sem.at[slot, xx], along_z(step, xx)).wait_recv()

    for slot, step in enumerate(near):
        for d in (2, 1, 3, 0):
            first(slot, step, (x + d) % 4).start()
    for d in range(1, 4):
        first(4, 0, (x + d) % 4).start()
    kraw[z, x] = ksend[x]

    def rows_of(mm):
        return modes_ref.at[pl.ds(mm * 8, 8)]

    fs[...] = jnp.ones_like(fs)
    fs[0:18, 0:64] = freq_ref[...]
    for d in range(1, 8):
        mm = (me + d) % 8
        remote(rows_of(mm), mrecv.at[me], ms_sem.at[mm], mr_sem.at[me], at(x, mm)).start()
        remote(fs, frecv.at[me], fs_sem.at[mm], fr_sem.at[me], at(x, mm)).start()
    own_modes = pltpu.make_async_copy(rows_of(me), mrecv.at[me], c_sem.at[4])
    own_modes.start()
    frecv[me] = fs[...]

    qs[...] = jnp.zeros_like(qs)
    qs[0:3, 0:64] = qp_ref[...].astype(F32)
    points = dot_t(first_ref[...], qs[...].astype(BF)).astype(BF)
    inner = dot(points, lattice_ref[...]).astype(jnp.int32) & 31
    angle = inner.astype(F32) * (TWO_PI / 32)
    ph[x, 0:64, :] = jnp.cos(angle).astype(BF)
    ph[x, 64:128, :] = jnp.sin(angle).astype(BF)

    def hop(offset, step, part):
        spot = (offset - step) % nz
        piece = kraw.at[(z + nz + offset) % nz, pl.ds(part * 2, 2)]
        return remote(piece, piece, zs_sem.at[spot, part], zr_sem.at[spot, part], along_z(step))

    def came(offset, part):
        if offset in (-3, 3):
            slot = near.index(-offset)
            for xx in (part * 2, part * 2 + 1):
                first_came(slot, -offset, xx)
        else:
            hop(offset, 0, part).wait_recv()

    routes = {-3: (3, 1, -1), 3: (-3, 1, -1), -6: (1, -1), 6: (1, -1)}

    def pass_on(one, other):
        for part in range(2):
            for offset in (one, other):
                came(offset, part)
                for step in routes[offset]:
                    hop(offset, step, part).start()
                if (offset, part) in ((-6, 0), (6, 1)):
                    hop(offset, 2 if part == 0 else -2, part).start()

    def assemble(offset):
        shard = (z + nz + offset) % nz
        kbuf[shard] = dot(gather_ref[...], kraw[shard].reshape(320, 128)).astype(BF)

    for d in range(1, 4):
        xx = (x + d) % 4
        remote(ph.at[x], ph.at[x], ps_sem.at[xx], pr_sem.at[x], at(xx, me)).start()

    @pl.loop(0, 32)
    def _(i):
        both = [rotq_ref[pl.ds(pl.multiple_of(ri * 1024 + i * 32, 32), 32), :] for ri in range(2)]
        flipped = dot_t(second_ref[...], jnp.concatenate(both, axis=0))
        for q4 in range(4):
            xf[q4, pl.ds(i, 16, stride=32), :] = flipped[q4 * 16:(q4 + 1) * 16]

    lane_m = lax.broadcasted_iota(jnp.int32, (256, 128), 1) % 16
    for t in range(8):
        chosen = jnp.where((shift_ref[...] == ws_ref[t]) & (lane_m < wc_ref[t]), 1.0, 0.0).astype(BF)
        cut = jnp.zeros((64, 128), F32)
        for q4 in range(4):
            cut = cut + dot(xf[q4, t * 64:(t + 1) * 64, :].astype(BF), chosen[q4 * 64:(q4 + 1) * 64])
        win[x, 0, t * 32:(t + 1) * 32, :] = cut[0:32].astype(BF)
        win[x, 1, t * 32:(t + 1) * 32, :] = cut[32:64].astype(BF)
    for d in range(1, 4):
        xx = (x + d) % 4
        remote(win.at[x], win.at[x], ns_sem.at[xx], nr_sem.at[x], at(xx, me)).start()

    def weights(xx):
        for par in range(2):
            for q4 in range(4):
                spreaded = dot(win[xx, par], spread_ref[par, :, q4 * 512:(q4 + 1) * 512]).astype(BF)
                for g in range(4):
                    rows = spreaded[:, g * 128:(g + 1) * 128].reshape(8, 32, 128)
                    start = par * 128 + g * 32
                    wq[pl.ds(xx * 8, 8), q4, start:start + 32, :] = rows

    row_q = sum((lax.broadcasted_iota(jnp.int32, (144, 128), 0) >= 18 * n).astype(jnp.int32) for n in range(1, 8))
    diagonal = lax.broadcasted_iota(jnp.int32, (144, 128), 1) == row_q + me * 8

    def vectors(mm):
        own = 1.0 / jnp.sqrt(2.0 * frecv[mm])
        high = own.astype(BF)
        rest = own - high.astype(F32)
        middle = rest.astype(BF)
        low = (rest - middle.astype(F32)).astype(BF)
        by_row = dot(rowmode_ref[...], high) + dot(rowmode_ref[...], middle) + dot(rowmode_ref[...], low)
        scale[mm] = jnp.sum(jnp.where(diagonal, by_row, 0.0), axis=1, keepdims=True)
        rows = mrecv[mm].reshape(288, 144)
        mf[0] = rows[:, :128].astype(F32)
        mf[1, :, 0:16] = rows[:, 128:].astype(F32)
        for ri in range(2):
            halves = [mf[n, pl.ds(ri, 144, stride=2), :].astype(BF) for n in range(2)]
            spreaded = dot(jnp.concatenate(halves, axis=1), pick_ref[...]).astype(BF)
            for par in range(2):
                start = (par * 2 + ri) * 640
                lhs[mm, :, start:start + 640] = spreaded * mask_ref[par]

    def wait_window(xx):
        remote(win.at[xx], win.at[xx], ns_sem.at[xx], nr_sem.at[xx], at(xx, me)).wait_recv()

    def wait_vectors(mm):
        remote(rows_of(mm), mrecv.at[mm], ms_sem.at[mm], mr_sem.at[mm], at(x, mm)).wait_recv()
        remote(fs, frecv.at[mm], fs_sem.at[mm], fr_sem.at[mm], at(x, mm)).wait_recv()

    pass_on(-3, 3)
    for copy in constant[:3]:
        copy.wait()
    own_modes.wait()
    weights(x)
    vectors(me)
    pass_on(-6, 6)
    for offset in (-3, 3, -6, 6):
        assemble(offset)
    for d in range(1, 4):
        wait_window((x + d) % 4)
        weights((x + d) % 4)
    for d in range(1, 4):
        first_came(4, 0, (x + d) % 4)
    assemble(0)
    for slot, step in ((2, 1), (3, -1)):
        for xx in range(4):
            first_came(slot, step, xx)
        assemble(-step)
    for d in range(1, 8):
        wait_vectors((me + d) % 8)
        vectors((me + d) % 8)
    for offset in (-2, 2, -4, 4, -5, 5, -7, 7, 8):
        for part in range(2):
            came(offset, part)
        assemble(offset)

    for d in range(1, 4):
        xx = (x + d) % 4
        remote(ph.at[xx], ph.at[xx], ps_sem.at[xx], pr_sem.at[xx], at(xx, me)).wait_recv()
    turn = lax.broadcasted_iota(jnp.int32, (64, 128), 1) < 64

    def sum_pair(cp):
        pair = [
            kbuf[:, pl.ds(pl.multiple_of((cp * 2 + p) * 16, 16), 16), :].reshape(nr, 128) for p in range(2)
        ]
        both = dot(ph[...].reshape(512, nr), jnp.concatenate(pair, axis=1))
        for p in range(2):
            for xx in range(4):
                along = both[xx * 128:xx * 128 + 64, p * 128:(p + 1) * 128]
                across = pltpu.roll(both[xx * 128 + 64:xx * 128 + 128, p * 128:(p + 1) * 128], 64, 1)
                total = along + jnp.where(turn, -across, across)
                for par in range(2):
                    qbuf[par, pl.ds(xx * 640 + cp * 2 + p, 32, stride=20), :] = total[par * 32:(par + 1) * 32]

    @pl.loop(0, 3)
    def _(third):
        for u in range(3):
            sum_pair(third * 3 + u)

    row = lax.broadcasted_iota(jnp.int32, (80, 256), 0)

    def band(xx, mm):
        spot = xx * 8 + mm
        rows = pl.ds(pl.multiple_of(spot * 80, 80), 80)
        own = jnp.concatenate([qbuf[0, rows, :], qbuf[1, rows, :]], axis=1)
        wide = [
            jnp.where((row >= q4 * 20) & (row < q4 * 20 + 20), own, 0.0).astype(BF) for q4 in range(4)
        ]
        return dot(jnp.concatenate(wide, axis=1), wq[spot].reshape(1024, 128)).astype(BF)

    def block(xx, mm, sx, sm):
        return remote(
            bsend.at[xx * 8 + mm], brecv.at[sx, sm], bs_sem.at[xx * 8 + mm], br_sem.at[sx * 8 + sm], at(xx, mm)
        )

    @pl.loop(0, 3)
    def _(n):
        xx = (x + 2 - n + n // 2 * 3) % 4
        for half in range(2):
            for mm in range(half * 4, half * 4 + 4):
                bsend[xx * 8 + mm] = band(xx, mm)
            for mm in range(half * 4, half * 4 + 4):
                block(xx, mm, x, me).start()

    for d in range(1, 8):
        bsend[x * 8 + (me + d) % 8] = band(x, (me + d) % 8)
        block(x, (me + d) % 8, x, me).start()
    brecv[x, me] = band(x, me)

    constant[3].wait()
    for d in (0, 1, 3, 2):
        xx = (x + d) % 4

        @pl.loop(1 if d == 0 else 0, 8)
        def _(n):
            block(xx, (me + n) % 8, xx, (me + n) % 8).wait_recv()

        placed = dot(brecv[xx].reshape(640, 128), order_ref[pl.ds(pl.multiple_of(xx * 128, 128), 128), :]).astype(BF)
        for part in range(4):
            here = placed[:, part * 256:(part + 1) * 256]
            if d > 0:
                here = here + rhs[part * 640:(part + 1) * 640, :]
            rhs[part * 640:(part + 1) * 640, :] = here

    def finish(chip):
        done = dot(lhs[pl.ds(chip * 2, 2)].reshape(288, 2560), rhs[...])
        for n in range(2):
            one = done[n * 144:(n + 1) * 144] * scale[chip * 2 + n]
            for ri in range(2):
                of[n, pl.ds(ri, 144, stride=2), :] = one[:, ri * 128:(ri + 1) * 128]
            osend[chip * 2 + n] = of[n].astype(BF)

    def send_out(mm):
        remote(osend.at[mm], o_ref.at[me], os_sem.at[mm], or_sem.at[me], at(x, mm)).start()

    for d in (2, 1, 3):
        chip = (me // 2 + d) % 4
        finish(chip)
        send_out(chip * 2 + me % 2)
        send_out(chip * 2 + 1 - me % 2)
    finish(me // 2)
    send_out(me // 2 * 2 + 1 - me % 2)
    o_ref[me] = osend[me]

    @pl.loop(1, 8)
    def _(d):
        mm = (me + d) % 8
        remote(osend.at[mm], o_ref.at[mm], os_sem.at[mm], or_sem.at[mm], at(x, mm)).wait()

    for slot, step in enumerate(near):
        for xx in range(4):
            first(slot, step, xx).wait_send()
    for d in range(1, 4):
        xx = (x + d) % 4
        first(4, 0, xx).wait_send()
        remote(ph.at[x], ph.at[x], ps_sem.at[xx], pr_sem.at[x], at(xx, me)).wait_send()
        remote(win.at[x], win.at[x], ns_sem.at[xx], nr_sem.at[x], at(xx, me)).wait_send()
    for d in range(1, 8):
        mm = (me + d) % 8
        remote(rows_of(mm), mrecv.at[me], ms_sem.at[mm], mr_sem.at[me], at(x, mm)).wait_send()
        remote(fs, frecv.at[me], fs_sem.at[mm], fr_sem.at[me], at(x, mm)).wait_send()
    for part in range(2):
        for offset, steps in routes.items():
            for step in steps:
                hop(offset, step, part).wait_send()
    hop(-6, 2, 0).wait_send()
    hop(6, -2, 1).wait_send()

    @pl.loop(1, 32)
    def _(d):
        xx, mm = (x + d // 8) % 4, (me + d) % 8
        block(xx, mm, x, me).wait_send()


def shards(g_wann, rot_k, qpoints, rot_kq, win_count, win_start, modes_vec, frequencies):
    nz = lax.axis_size("pb") // NX
    small, large = constants(nz)

    g_rows = g_wann.reshape(4, 2, 18, 8, 128).transpose(0, 2, 3, 1, 4).reshape(1152, 128)
    rot = rot_k.transpose(0, 2, 1)
    rotq = rot_kq.transpose(1, 2, 3, 0).reshape(2048, 64)
    freq = frequencies.T
    modes = modes_vec.transpose(0, 2, 1, 3)

    vmem = pl.BlockSpec(memory_space=pltpu.VMEM)
    smem = pl.BlockSpec(memory_space=pltpu.SMEM)
    whole = pl.BlockSpec(memory_space=pl.ANY)
    sem = pltpu.SemaphoreType.DMA
    out = pl.pallas_call(
        functools.partial(kernel, nz),
        out_shape=jax.ShapeDtypeStruct((8, 288, 128), BF),
        in_specs=[smem, smem] + [vmem] * 5 + [whole] + [vmem] * 7 + [whole] * 4,
        out_specs=vmem,
        scratch_shapes=[
            pltpu.VMEM((2, 128, 2048), BF),
            pltpu.VMEM((256, 640), BF),
            pltpu.VMEM((2, 144, 640), BF),
            pltpu.VMEM((512, 1024), BF),
            pltpu.VMEM((1152, 128), F32),
            pltpu.VMEM((80, 2048), BF),
            pltpu.VMEM((2048, 512), BF),
            pltpu.VMEM((80, 512), F32),
            pltpu.VMEM((8, 128), F32),
            pltpu.VMEM((24, 128), F32),
            pltpu.VMEM((4, 80, 128), F32),
            pltpu.VMEM((4, 80, 128), BF),
            pltpu.VMEM((nz, 4, 80, 128), BF),
            pltpu.VMEM((nz, 288, 128), BF),
            pltpu.VMEM((4, 128, nz * 16), BF),
            pltpu.VMEM((4, 512, 64), F32),
            pltpu.VMEM((4, 2, 256, 128), BF),
            pltpu.VMEM((32, 4, 256, 128), BF),
            pltpu.VMEM((2, 2560, 128), F32),
            pltpu.VMEM((32, 80, 128), BF),
            pltpu.VMEM((4, 8, 80, 128), BF),
            pltpu.VMEM((8, 8, 18, 2, 144), BF),
            pltpu.VMEM((2, 288, 128), F32),
            pltpu.VMEM((8, 24, 128), F32),
            pltpu.VMEM((8, 144, 2560), BF),
            pltpu.VMEM((8, 144, 1), F32),
            pltpu.VMEM((2560, 256), BF),
            pltpu.VMEM((2, 288, 128), F32),
            pltpu.VMEM((8, 288, 128), BF),
            sem((5,)),
            sem((5, 4)), sem((5, 4)), sem((4,)), sem((4,)), sem((4,)), sem((4,)), sem((8,)), sem((8,)), sem((8,)), sem((8,)),
            sem((16, 2)), sem((16, 2)), sem((32,)), sem((32,)), sem((8,)), sem((8,)),
        ],
        compiler_params=pltpu.CompilerParams(
            collective_id=0, has_side_effects=True, vmem_limit_bytes=56 * 1024 * 1024
        ),
    )(win_start, win_count, g_rows, rot, qpoints, rotq, freq, modes, *small, *large)
    return out.reshape(64, 18, 2, 128).transpose(0, 2, 1, 3)


def solution(mesh):
    placed = (
        P("pb", None, "mode", None),
        P(),
        P(None, "pb"),
        P("pb", None, None, None),
        P("pb"),
        P("pb"),
        P("pb", None, "mode", None),
        P("pb", "mode"),
    )
    return jax.shard_map(
        shards, mesh=mesh, in_specs=placed, out_specs=P("pb", None, "mode", None), check_vma=False
    )
```

```python
import functools
import jax
import jax.numpy as jnp
import numpy as np
from jax import lax
from jax.experimental import pallas as pl
from jax.experimental.pallas import tpu as pltpu
from jax.sharding import PartitionSpec as P

NX = 4
NM = 8
TWO_PI = 6.283185307179586
BF = jnp.bfloat16
F32 = jnp.float32


def dot(a, b):
    return jnp.dot(a, b, preferred_element_type=F32)


def dot_t(a, b):
    return lax.dot_general(a, b, (((1,), (1,)), ((), ())), preferred_element_type=F32)


def constants(nz):
    rows = np.arange(nz * 16)
    z, x, r4 = rows // 16, rows // 4 % 4, rows % 4
    r = (x * nz + z) * 4 + r4
    lattice = np.zeros((8, nz * 16), np.float32)
    lattice[0] = r % 8 - 4
    lattice[1] = r // 8 % 8 - 4
    lattice[2] = r // 64 - 4

    row, lane = np.arange(256)[:, None], np.arange(128)[None, :]
    same = row // 32 == lane // 16
    shift = np.where(same, row % 32 - lane % 16, -1000).astype(np.int32)

    spread = np.zeros((2, 4, 2, 16, 4, 2, 2, 2, 2, 16, 2), np.float32)
    for par in range(2):
        for q4 in range(4):
            for m in range(16):
                for b in range(2):
                    spread[par, q4, 0, m, q4, 0, b, par, 0, m, b] = 1
                    spread[par, q4, 1, m, q4, 1, b, par, 0, m, b] = 1
                    spread[par, q4, 1, m, q4, 0, b, par, 1, m, b] = -1
                    spread[par, q4, 0, m, q4, 1, b, par, 1, m, b] = 1
    spread = spread.reshape(2, 128, 2048)

    pick = np.zeros((256, 640), np.float32)
    for c in range(144):
        for q4 in range(4):
            pick[c, c // 18 * 80 + q4 * 20 + c % 18] = 1
    mask = np.zeros((2, 2, 4, 18, 8, 4, 20), np.float32)
    for par in range(2):
        for q4 in range(4):
            mask[par, par, q4, :, :, q4, :] = 1
    mask = mask.reshape(2, 144, 640)

    order = np.zeros((4, 2, 2, 16, 2, 2, 2, 2, 16, 8), np.float32)
    for xx in range(4):
        for par in range(2):
            for m in range(16):
                for b in range(2):
                    order[xx, par, 0, m, b, par, 0, 0, m, xx * 2 + b] = 1
                    order[xx, par, 1, m, b, par, 0, 1, m, xx * 2 + b] = 1
                    order[xx, par, 1, m, b, par, 1, 0, m, xx * 2 + b] = -1
                    order[xx, par, 0, m, b, par, 1, 1, m, xx * 2 + b] = 1
    order = order.reshape(512, 1024)

    bands = np.zeros((8, 4, 2, 2, 32), np.float32)
    for xx in range(4):
        for b in range(2):
            bands[xx * 2 + b, xx, :, b, :] = 1
    bands = bands.reshape(8, 512)

    q = np.arange(64)
    first = np.zeros((64, 128), np.float32)
    first[q, q // 4 % 8 * 8 + q // 32 * 4 + q % 4] = 1
    second = np.zeros((64, 64), np.float32)
    second[q, q // 2 % 8 * 8 + q % 2 * 4 + q // 16] = 1

    gather = np.zeros((18, 4, 4, 4, 80), np.float32)
    for c in range(18):
        for xx in range(4):
            for r4 in range(4):
                gather[c, xx, r4, xx, c * 4 + r4] = 1
    gather = gather.reshape(288, 320)

    modes = np.zeros((144, 24), np.float32)
    modes[np.arange(144), np.arange(144) % 18] = 1
    half = lambda a: jnp.asarray(a, BF)
    small = [half(lattice), jnp.asarray(shift), half(bands), half(first), half(second), half(modes), half(gather)]
    return small, [half(spread), half(pick), half(mask), half(order)]


def kernel(
    nz, ws_ref, wc_ref, g_ref, rot_ref, qp_ref, rotq_ref, freq_ref, modes_ref,
    lattice_ref, shift_ref, bands_ref, first_ref, second_ref, rowmode_ref, gather_ref, spread_in, pick_in, mask_in, order_in, o_ref,
    spread_ref, pick_ref, mask_ref, order_ref,
    gf, gl, kw, tf, qs, fs, kf, ksend, kraw, kbuf, ph, xf, win, wq, qbuf, bsend, brecv, mrecv, mf, frecv, lhs, scale, rhs,
    of, osend, c_sem,
    ks_sem, kr_sem, ps_sem, pr_sem, ns_sem, nr_sem, ms_sem, mr_sem, fs_sem, fr_sem, zs_sem, zr_sem, bs_sem, br_sem,
    os_sem, or_sem,
):
    me = lax.axis_index("mode")
    pb = lax.axis_index("pb")
    x, z = pb // nz, pb % nz
    nr = nz * 16

    def at(xx, mm):
        return {"mode": mm, "pb": xx * nz + z}

    def remote(src, dst, ssem, rsem, where):
        return pltpu.make_async_remote_copy(
            src_ref=src, dst_ref=dst, send_sem=ssem, recv_sem=rsem,
            device_id=where, device_id_type=pl.DeviceIdType.MESH,
        )

    def along_z(step, xx=None):
        return {"mode": me, "pb": (x if xx is None else xx) * nz + (z + nz + step) % nz}

    barrier = pltpu.get_barrier_semaphore()

    @pl.loop(1, 32)
    def _(d):
        pl.semaphore_signal(
            barrier, inc=1, device_id=at((x + d // 8) % 4, (me + d) % 8), device_id_type=pl.DeviceIdType.MESH
        )

    near = (3, -3, 1, -1)
    for step in near:
        for xx in range(4):
            pl.semaphore_signal(barrier, inc=1, device_id=along_z(step, xx), device_id_type=pl.DeviceIdType.MESH)
    for step in (2, -2):
        pl.semaphore_signal(barrier, inc=1, device_id=along_z(step), device_id_type=pl.DeviceIdType.MESH)

    qbuf[...] = jnp.zeros_like(qbuf)
    mf[...] = jnp.zeros_like(mf)
    constant = [
        pltpu.make_async_copy(source, held, c_sem.at[n])
        for n, (source, held) in enumerate(
            ((spread_in, spread_ref), (pick_in, pick_ref), (mask_in, mask_ref), (order_in, order_ref))
        )
    ]
    for copy in constant:
        copy.start()

    lane = lax.broadcasted_iota(jnp.int32, (32, 512), 1)
    lane_i = lane % 32
    turn_b = lambda ri: lax.dot_general(
        rot_ref[ri], bands_ref[...], (((0,), (0,)), ((), ())), preferred_element_type=F32
    )
    real, imag = turn_b(0), turn_b(1)
    in_real = lane % 128 < 64
    parts = (jnp.where(in_real, real, imag).astype(BF), jnp.where(in_real, -imag, real).astype(BF))
    for ri in range(2):
        part = parts[ri]

        @pl.loop(0, 32)
        def _(i):
            kw[pl.ds(pl.multiple_of(ri * 1024 + i * 32, 32), 32), :] = jnp.where(lane_i == i, part, 0.0).astype(BF)

    gf[...] = g_ref[...].astype(F32)
    for ri in range(2):
        for k in range(8):
            block = (ri * 8 + k) * 128
            gl[0:72, block:block + 128] = gf[pl.ds(k * 2 + ri, 72, stride=16), :].astype(BF)
    tf[...] = dot(gl[...], kw[...])
    kf[...] = jnp.zeros_like(kf)
    for xx in range(4):
        for r in range(4):
            kf[xx, pl.ds(r, 18, stride=4), :] = tf[r * 18:r * 18 + 18, xx * 128:(xx + 1) * 128]
    ksend[...] = kf[...].astype(BF)

    pl.semaphore_wait(barrier, 31 + 4 * len(near) + 2)

    def first(slot, step, xx):
        return remote(ksend.at[xx], kraw.at[slot, x], ks_sem.at[slot, xx], kr_sem.at[slot, x], along_z(step, xx))

    def first_came(slot, step, xx):
        remote(ksend.at[xx], kraw.at[slot, xx], ks_sem.at[slot, xx], kr_sem.at[slot, xx], along_z(step, xx)).wait_recv()

    for slot, step in enumerate(near):
        for d in (2, 1, 3, 0):
            first(slot, step, (x + d) % 4).start()
    for d in range(1, 4):
        first(4, 0, (x + d) % 4).start()
    kraw[4, x] = ksend[x]

    def rows_of(mm):
        return modes_ref.at[pl.ds(mm * 8, 8)]

    fs[...] = jnp.ones_like(fs)
    fs[0:18, 0:64] = freq_ref[...]
    for d in range(1, 8):
        mm = (me + d) % 8
        remote(rows_of(mm), mrecv.at[me], ms_sem.at[mm], mr_sem.at[me], at(x, mm)).start()
        remote(fs, frecv.at[me], fs_sem.at[mm], fr_sem.at[me], at(x, mm)).start()
    own_modes = pltpu.make_async_copy(rows_of(me), mrecv.at[me], c_sem.at[4])
    own_modes.start()
    frecv[me] = fs[...]

    qs[...] = jnp.zeros_like(qs)
    qs[0:3, 0:64] = qp_ref[...].astype(F32)
    points = dot_t(first_ref[...], qs[...].astype(BF)).astype(BF)
    inner = dot(points, lattice_ref[...]).astype(jnp.int32) & 31
    angle = inner.astype(F32) * (TWO_PI / 32)
    ph[x, 0:64, :] = jnp.cos(angle).astype(BF)
    ph[x, 64:128, :] = jnp.sin(angle).astype(BF)

    def hop(offset, step, part):
        spot = (offset - step) % nz
        piece = kbuf.at[(z + nz + offset) % nz, pl.ds(part * 144, 144)]
        return remote(piece, piece, zs_sem.at[spot, part], zr_sem.at[spot, part], along_z(step))

    def came(offset, part):
        hop(offset, 0, part).wait_recv()

    def assemble(slot, step):
        for xx in range(4):
            first_came(slot, step, xx)
        kbuf[(z + nz - step) % nz] = dot(gather_ref[...], kraw[slot].reshape(320, 128)).astype(BF)

    routes = {-3: (3, 1, -1), 3: (-3, 1, -1), -6: (1, -1), 6: (1, -1)}

    for d in range(1, 4):
        xx = (x + d) % 4
        remote(ph.at[x], ph.at[x], ps_sem.at[xx], pr_sem.at[x], at(xx, me)).start()

    @pl.loop(0, 32, unroll=4)
    def _(i):
        both = [rotq_ref[pl.ds(pl.multiple_of(ri * 1024 + i * 32, 32), 32), :] for ri in range(2)]
        flipped = dot_t(second_ref[...], jnp.concatenate(both, axis=0))
        for q4 in range(4):
            xf[q4, pl.ds(i, 16, stride=32), :] = flipped[q4 * 16:(q4 + 1) * 16]

    assemble(0, 3)
    assemble(1, -3)
    for part in range(2):
        hop(-3, 3, part).start()
        hop(3, -3, part).start()
    for part in range(2):
        for offset in (-3, 3):
            for step in (1, -1):
                hop(offset, step, part).start()

    lane_m = lax.broadcasted_iota(jnp.int32, (256, 128), 1) % 16
    for t in range(8):
        chosen = jnp.where((shift_ref[...] == ws_ref[t]) & (lane_m < wc_ref[t]), 1.0, 0.0).astype(BF)
        cut = jnp.zeros((64, 128), F32)
        for q4 in range(4):
            cut = cut + dot(xf[q4, t * 64:(t + 1) * 64, :].astype(BF), chosen[q4 * 64:(q4 + 1) * 64])
        win[x, 0, t * 32:(t + 1) * 32, :] = cut[0:32].astype(BF)
        win[x, 1, t * 32:(t + 1) * 32, :] = cut[32:64].astype(BF)
    for d in range(1, 4):
        xx = (x + d) % 4
        remote(win.at[x], win.at[x], ns_sem.at[xx], nr_sem.at[x], at(xx, me)).start()

    def weights(xx):
        for par in range(2):
            for q4 in range(4):
                spreaded = dot(win[xx, par], spread_ref[par, :, q4 * 512:(q4 + 1) * 512]).astype(BF)
                for g in range(4):
                    rows = spreaded[:, g * 128:(g + 1) * 128].reshape(8, 32, 128)
                    start = par * 128 + g * 32
                    wq[pl.ds(xx * 8, 8), q4, start:start + 32, :] = rows

    row_q = sum((lax.broadcasted_iota(jnp.int32, (144, 128), 0) >= 18 * n).astype(jnp.int32) for n in range(1, 8))
    diagonal = lax.broadcasted_iota(jnp.int32, (144, 128), 1) == row_q + me * 8

    def vectors(mm):
        own = 1.0 / jnp.sqrt(2.0 * frecv[mm])
        high = own.astype(BF)
        rest = own - high.astype(F32)
        middle = rest.astype(BF)
        low = (rest - middle.astype(F32)).astype(BF)
        by_row = dot(rowmode_ref[...], high) + dot(rowmode_ref[...], middle) + dot(rowmode_ref[...], low)
        scale[mm] = jnp.sum(jnp.where(diagonal, by_row, 0.0), axis=1, keepdims=True)
        rows = mrecv[mm].reshape(288, 144)
        mf[0] = rows[:, :128].astype(F32)
        mf[1, :, 0:16] = rows[:, 128:].astype(F32)
        for ri in range(2):
            halves = [mf[n, pl.ds(ri, 144, stride=2), :].astype(BF) for n in range(2)]
            spreaded = dot(jnp.concatenate(halves, axis=1), pick_ref[...]).astype(BF)
            for par in range(2):
                start = (par * 2 + ri) * 640
                lhs[mm, :, start:start + 640] = spreaded * mask_ref[par]

    def wait_window(xx):
        remote(win.at[xx], win.at[xx], ns_sem.at[xx], nr_sem.at[xx], at(xx, me)).wait_recv()

    def wait_vectors(mm):
        remote(rows_of(mm), mrecv.at[mm], ms_sem.at[mm], mr_sem.at[mm], at(x, mm)).wait_recv()
        remote(fs, frecv.at[mm], fs_sem.at[mm], fr_sem.at[mm], at(x, mm)).wait_recv()

    for copy in constant[:3]:
        copy.wait()
    own_modes.wait()
    weights(x)
    for part in range(2):
        for offset in (-6, 6):
            came(offset, part)
            for step in (1, -1):
                hop(offset, step, part).start()
            if (offset, part) in ((-6, 0), (6, 1)):
                hop(offset, 2 if part == 0 else -2, part).start()
    vectors(me)
    for d in range(1, 4):
        wait_window((x + d) % 4)
        weights((x + d) % 4)
    for d in range(1, 8):
        wait_vectors((me + d) % 8)
        vectors((me + d) % 8)
    for d in range(1, 4):
        first_came(4, 0, (x + d) % 4)
    kbuf[z] = dot(gather_ref[...], kraw[4].reshape(320, 128)).astype(BF)
    assemble(2, 1)
    assemble(3, -1)
    for offset in (-2, 2, -4, 4, -5, 5, -7, 7, 8):
        for part in range(2):
            came(offset, part)

    for d in range(1, 4):
        xx = (x + d) % 4
        remote(ph.at[xx], ph.at[xx], ps_sem.at[xx], pr_sem.at[xx], at(xx, me)).wait_recv()
    turn = lax.broadcasted_iota(jnp.int32, (64, 128), 1) < 64

    def sums(xx):
        for cp in range(9):
            pair = [kbuf[:, (cp * 2 + p) * 16:(cp * 2 + p) * 16 + 16, :].reshape(nr, 128) for p in range(2)]
            both = dot(ph[xx], jnp.concatenate(pair, axis=1))
            for p in range(2):
                along = both[0:64, p * 128:(p + 1) * 128]
                across = pltpu.roll(both[64:128, p * 128:(p + 1) * 128], 64, 1)
                total = along + jnp.where(turn, -across, across)
                for par in range(2):
                    qbuf[par, pl.ds(xx * 640 + cp * 2 + p, 32, stride=20), :] = total[par * 32:(par + 1) * 32]

    row = lax.broadcasted_iota(jnp.int32, (80, 256), 0)

    def band(xx, mm):
        spot = xx * 8 + mm
        rows = pl.ds(pl.multiple_of(spot * 80, 80), 80)
        own = jnp.concatenate([qbuf[0, rows, :], qbuf[1, rows, :]], axis=1)
        wide = [
            jnp.where((row >= q4 * 20) & (row < q4 * 20 + 20), own, 0.0).astype(BF) for q4 in range(4)
        ]
        return dot(jnp.concatenate(wide, axis=1), wq[spot].reshape(1024, 128)).astype(BF)

    def block(xx, mm, sx, sm):
        return remote(
            bsend.at[xx * 8 + mm], brecv.at[sx, sm], bs_sem.at[xx * 8 + mm], br_sem.at[sx * 8 + sm], at(xx, mm)
        )

    @pl.loop(0, 3)
    def _(n):
        xx = (x + 2 - n + n // 2 * 3) % 4
        sums(xx)
        for half in range(2):
            for mm in range(half * 4, half * 4 + 4):
                bsend[xx * 8 + mm] = band(xx, mm)
            for mm in range(half * 4, half * 4 + 4):
                block(xx, mm, x, me).start()

    sums(x)
    for d in range(1, 8):
        bsend[x * 8 + (me + d) % 8] = band(x, (me + d) % 8)
        block(x, (me + d) % 8, x, me).start()
    brecv[x, me] = band(x, me)

    constant[3].wait()
    for d in (0, 1, 3, 2):
        xx = (x + d) % 4

        @pl.loop(1 if d == 0 else 0, 8)
        def _(n):
            block(xx, (me + n) % 8, xx, (me + n) % 8).wait_recv()

        placed = dot(brecv[xx].reshape(640, 128), order_ref[pl.ds(pl.multiple_of(xx * 128, 128), 128), :]).astype(BF)
        for part in range(4):
            here = placed[:, part * 256:(part + 1) * 256]
            if d > 0:
                here = here + rhs[part * 640:(part + 1) * 640, :]
            rhs[part * 640:(part + 1) * 640, :] = here

    def finish(chip):
        done = dot(lhs[pl.ds(chip * 2, 2)].reshape(288, 2560), rhs[...])
        for n in range(2):
            one = done[n * 144:(n + 1) * 144] * scale[chip * 2 + n]
            for ri in range(2):
                of[n, pl.ds(ri, 144, stride=2), :] = one[:, ri * 128:(ri + 1) * 128]
            osend[chip * 2 + n] = of[n].astype(BF)

    def send_out(mm):
        remote(osend.at[mm], o_ref.at[me], os_sem.at[mm], or_sem.at[me], at(x, mm)).start()

    for d in (2, 1, 3):
        chip = (me // 2 + d) % 4
        finish(chip)
        send_out(chip * 2 + me % 2)
        send_out(chip * 2 + 1 - me % 2)
    finish(me // 2)
    send_out(me // 2 * 2 + 1 - me % 2)
    o_ref[me] = osend[me]

    @pl.loop(1, 8)
    def _(d):
        mm = (me + d) % 8
        remote(osend.at[mm], o_ref.at[mm], os_sem.at[mm], or_sem.at[mm], at(x, mm)).wait()

    for slot, step in enumerate(near):
        for xx in range(4):
            first(slot, step, xx).wait_send()
    for d in range(1, 4):
        xx = (x + d) % 4
        first(4, 0, xx).wait_send()
        remote(ph.at[x], ph.at[x], ps_sem.at[xx], pr_sem.at[x], at(xx, me)).wait_send()
        remote(win.at[x], win.at[x], ns_sem.at[xx], nr_sem.at[x], at(xx, me)).wait_send()
    for d in range(1, 8):
        mm = (me + d) % 8
        remote(rows_of(mm), mrecv.at[me], ms_sem.at[mm], mr_sem.at[me], at(x, mm)).wait_send()
        remote(fs, frecv.at[me], fs_sem.at[mm], fr_sem.at[me], at(x, mm)).wait_send()
    for part in range(2):
        for offset, steps in routes.items():
            for step in steps:
                hop(offset, step, part).wait_send()
    hop(-6, 2, 0).wait_send()
    hop(6, -2, 1).wait_send()

    @pl.loop(1, 32)
    def _(d):
        xx, mm = (x + d // 8) % 4, (me + d) % 8
        block(xx, mm, x, me).wait_send()


def shards(g_wann, rot_k, qpoints, rot_kq, win_count, win_start, modes_vec, frequencies):
    nz = lax.axis_size("pb") // NX
    small, large = constants(nz)

    g_rows = g_wann.reshape(4, 2, 18, 8, 128).transpose(0, 2, 3, 1, 4).reshape(1152, 128)
    rot = rot_k.transpose(0, 2, 1)
    rotq = rot_kq.transpose(1, 2, 3, 0).reshape(2048, 64)
    freq = frequencies.T
    modes = modes_vec.transpose(0, 2, 1, 3)

    vmem = pl.BlockSpec(memory_space=pltpu.VMEM)
    smem = pl.BlockSpec(memory_space=pltpu.SMEM)
    whole = pl.BlockSpec(memory_space=pl.ANY)
    sem = pltpu.SemaphoreType.DMA
    out = pl.pallas_call(
        functools.partial(kernel, nz),
        out_shape=jax.ShapeDtypeStruct((8, 288, 128), BF),
        in_specs=[smem, smem] + [vmem] * 5 + [whole] + [vmem] * 7 + [whole] * 4,
        out_specs=vmem,
        scratch_shapes=[
            pltpu.VMEM((2, 128, 2048), BF),
            pltpu.VMEM((256, 640), BF),
            pltpu.VMEM((2, 144, 640), BF),
            pltpu.VMEM((512, 1024), BF),
            pltpu.VMEM((1152, 128), F32),
            pltpu.VMEM((80, 2048), BF),
            pltpu.VMEM((2048, 512), BF),
            pltpu.VMEM((80, 512), F32),
            pltpu.VMEM((8, 128), F32),
            pltpu.VMEM((24, 128), F32),
            pltpu.VMEM((4, 80, 128), F32),
            pltpu.VMEM((4, 80, 128), BF),
            pltpu.VMEM((5, 4, 80, 128), BF),
            pltpu.VMEM((nz, 288, 128), BF),
            pltpu.VMEM((4, 128, nz * 16), BF),
            pltpu.VMEM((4, 512, 64), F32),
            pltpu.VMEM((4, 2, 256, 128), BF),
            pltpu.VMEM((32, 4, 256, 128), BF),
            pltpu.VMEM((2, 2560, 128), F32),
            pltpu.VMEM((32, 80, 128), BF),
            pltpu.VMEM((4, 8, 80, 128), BF),
            pltpu.VMEM((8, 8, 18, 2, 144), BF),
            pltpu.VMEM((2, 288, 128), F32),
            pltpu.VMEM((8, 24, 128), F32),
            pltpu.VMEM((8, 144, 2560), BF),
            pltpu.VMEM((8, 144, 1), F32),
            pltpu.VMEM((2560, 256), BF),
            pltpu.VMEM((2, 288, 128), F32),
            pltpu.VMEM((8, 288, 128), BF),
            sem((5,)),
            sem((5, 4)), sem((5, 4)), sem((4,)), sem((4,)), sem((4,)), sem((4,)), sem((8,)), sem((8,)), sem((8,)), sem((8,)),
            sem((16, 2)), sem((16, 2)), sem((32,)), sem((32,)), sem((8,)), sem((8,)),
        ],
        compiler_params=pltpu.CompilerParams(
            collective_id=0, has_side_effects=True, vmem_limit_bytes=56 * 1024 * 1024
        ),
    )(win_start, win_count, g_rows, rot, qpoints, rotq, freq, modes, *small, *large)
    return out.reshape(64, 18, 2, 128).transpose(0, 2, 1, 3)


def solution(mesh):
    placed = (
        P("pb", None, "mode", None),
        P(),
        P(None, "pb"),
        P("pb", None, None, None),
        P("pb"),
        P("pb"),
        P("pb", None, "mode", None),
        P("pb", "mode"),
    )
    return jax.shard_map(
        shards, mesh=mesh, in_specs=placed, out_specs=P("pb", None, "mode", None), check_vma=False
    )
```

```python
import functools
import jax
import jax.numpy as jnp
import numpy as np
from jax import lax
from jax.experimental import pallas as pl
from jax.experimental.pallas import tpu as pltpu
from jax.sharding import PartitionSpec as P

NX = 4
NM = 8
TWO_PI = 6.283185307179586
BF = jnp.bfloat16
F32 = jnp.float32


def dot(a, b):
    return jnp.dot(a, b, preferred_element_type=F32)


def dot_t(a, b):
    return lax.dot_general(a, b, (((1,), (1,)), ((), ())), preferred_element_type=F32)


def constants(nz):
    rows = np.arange(nz * 16)
    z, x, r4 = rows // 16, rows // 4 % 4, rows % 4
    r = (x * nz + z) * 4 + r4
    lattice = np.zeros((8, nz * 16), np.float32)
    lattice[0] = r % 8 - 4
    lattice[1] = r // 8 % 8 - 4
    lattice[2] = r // 64 - 4

    row, lane = np.arange(256)[:, None], np.arange(128)[None, :]
    same = row // 32 == lane // 16
    shift = np.where(same, row % 32 - lane % 16, -1000).astype(np.int32)

    spread = np.zeros((2, 4, 2, 16, 4, 2, 2, 2, 2, 16, 2), np.float32)
    for par in range(2):
        for q4 in range(4):
            for m in range(16):
                for b in range(2):
                    spread[par, q4, 0, m, q4, 0, b, par, 0, m, b] = 1
                    spread[par, q4, 1, m, q4, 1, b, par, 0, m, b] = 1
                    spread[par, q4, 1, m, q4, 0, b, par, 1, m, b] = -1
                    spread[par, q4, 0, m, q4, 1, b, par, 1, m, b] = 1
    spread = spread.reshape(2, 128, 2048)

    pick = np.zeros((256, 640), np.float32)
    for c in range(144):
        for q4 in range(4):
            pick[c, c // 18 * 80 + q4 * 20 + c % 18] = 1
    mask = np.zeros((4, 18, 8, 4, 20), np.float32)
    for q4 in range(4):
        mask[q4, :, :, q4, :] = 1
    mask = mask.reshape(72, 640)

    order = np.zeros((4, 2, 2, 16, 2, 2, 2, 2, 16, 8), np.float32)
    for xx in range(4):
        for par in range(2):
            for m in range(16):
                for b in range(2):
                    order[xx, par, 0, m, b, par, 0, 0, m, xx * 2 + b] = 1
                    order[xx, par, 1, m, b, par, 0, 1, m, xx * 2 + b] = 1
                    order[xx, par, 1, m, b, par, 1, 0, m, xx * 2 + b] = -1
                    order[xx, par, 0, m, b, par, 1, 1, m, xx * 2 + b] = 1
    order = order.reshape(512, 1024)

    bands = np.zeros((8, 4, 2, 2, 32), np.float32)
    for xx in range(4):
        for b in range(2):
            bands[xx * 2 + b, xx, :, b, :] = 1
    bands = bands.reshape(8, 512)

    q = np.arange(64)
    first = np.zeros((64, 128), np.float32)
    first[q, q // 4 % 8 * 8 + q // 32 * 4 + q % 4] = 1
    second = np.zeros((64, 64), np.float32)
    second[q, q // 2 % 8 * 8 + q % 2 * 4 + q // 16] = 1

    gather = np.zeros((18, 4, 4, 4, 80), np.float32)
    for c in range(18):
        for xx in range(4):
            for r4 in range(4):
                gather[c, xx, r4, xx, c * 4 + r4] = 1
    gather = gather.reshape(288, 320)

    modes = np.zeros((144, 24), np.float32)
    modes[np.arange(144), np.arange(144) % 18] = 1
    half = lambda a: jnp.asarray(a, BF)
    small = [half(lattice), jnp.asarray(shift), half(bands), half(first), half(second), half(modes), half(gather)]
    return small, [half(spread), half(pick), jnp.asarray(mask), half(order)]


def kernel(
    nz, ws_in, wc_in, g_in, rot_in, qp_in, rotq_in, freq_in, modes_ref,
    lattice_in, shift_in, bands_in, first_in, second_in, rowmode_in, gather_in, spread_in, pick_in, mask_in, order_in,
    o_ref,
    ws_ref, wc_ref, g_ref, rot_ref, qp_ref, rotq_ref, freq_ref,
    lattice_ref, shift_ref, bands_ref, first_ref, second_ref, rowmode_ref, gather_ref,
    spread_ref, pick_ref, mask_ref, order_ref,
    gf, gl, kw, tf, qs, fs, kf, ksend, kraw, kbuf, ph, xf, win, wq, qbuf, bsend, brecv, mrecv, mf, frecv, lhs, scale, rhs,
    of, osend, c_sem, i_sem,
    ks_sem, kr_sem, ps_sem, pr_sem, ns_sem, nr_sem, ms_sem, mr_sem, fs_sem, fr_sem, zs_sem, zr_sem, bs_sem, br_sem,
    os_sem, or_sem,
):
    me = lax.axis_index("mode")
    pb = lax.axis_index("pb")
    x, z = pb // nz, pb % nz
    nr = nz * 16

    def at(xx, mm):
        return {"mode": mm, "pb": xx * nz + z}

    def remote(src, dst, ssem, rsem, where):
        return pltpu.make_async_remote_copy(
            src_ref=src, dst_ref=dst, send_sem=ssem, recv_sem=rsem,
            device_id=where, device_id_type=pl.DeviceIdType.MESH,
        )

    def along_z(step, xx=None):
        return {"mode": me, "pb": (x if xx is None else xx) * nz + (z + nz + step) % nz}

    barrier = pltpu.get_barrier_semaphore()

    @pl.loop(1, 32)
    def _(d):
        pl.semaphore_signal(
            barrier, inc=1, device_id=at((x + d // 8) % 4, (me + d) % 8), device_id_type=pl.DeviceIdType.MESH
        )

    near = (3, -3, 1, -1)
    for step in near:
        for xx in range(4):
            pl.semaphore_signal(barrier, inc=1, device_id=along_z(step, xx), device_id_type=pl.DeviceIdType.MESH)
    for step in (2, -2):
        pl.semaphore_signal(barrier, inc=1, device_id=along_z(step), device_id_type=pl.DeviceIdType.MESH)

    fetched = [
        pltpu.make_async_copy(source, held, i_sem.at[n])
        for n, (source, held) in enumerate(
            (
                (g_in, g_ref), (rot_in, rot_ref), (bands_in, bands_ref), (ws_in, ws_ref), (wc_in, wc_ref),
                (qp_in, qp_ref), (rotq_in, rotq_ref), (freq_in, freq_ref), (lattice_in, lattice_ref),
                (shift_in, shift_ref), (first_in, first_ref), (second_in, second_ref), (rowmode_in, rowmode_ref),
                (gather_in, gather_ref),
            )
        )
    ]
    for copy in fetched:
        copy.start()
    qbuf[...] = jnp.zeros_like(qbuf)
    mf[...] = jnp.zeros_like(mf)
    constant = [
        pltpu.make_async_copy(source, held, c_sem.at[n])
        for n, (source, held) in enumerate(
            ((spread_in, spread_ref), (pick_in, pick_ref), (mask_in, mask_ref), (order_in, order_ref))
        )
    ]
    for copy in constant:
        copy.start()

    for copy in fetched[:3]:
        copy.wait()
    lane = lax.broadcasted_iota(jnp.int32, (32, 512), 1)
    lane_i = lane % 32
    turn_b = lambda ri: lax.dot_general(
        rot_ref[ri], bands_ref[...], (((0,), (0,)), ((), ())), preferred_element_type=F32
    )
    real, imag = turn_b(0), turn_b(1)
    in_real = lane % 128 < 64
    parts = (jnp.where(in_real, real, imag).astype(BF), jnp.where(in_real, -imag, real).astype(BF))
    for ri in range(2):
        part = parts[ri]

        @pl.loop(0, 32)
        def _(i):
            kw[pl.ds(pl.multiple_of(ri * 1024 + i * 32, 32), 32), :] = jnp.where(lane_i == i, part, 0.0).astype(BF)

    gf[...] = g_ref[...].astype(F32)
    for ri in range(2):
        for k in range(8):
            block = (ri * 8 + k) * 128
            gl[0:72, block:block + 128] = gf[pl.ds(k * 2 + ri, 72, stride=16), :].astype(BF)
    tf[...] = dot(gl[...], kw[...])
    kf[...] = jnp.zeros_like(kf)
    for xx in range(4):
        for r in range(4):
            kf[xx, pl.ds(r, 18, stride=4), :] = tf[r * 18:r * 18 + 18, xx * 128:(xx + 1) * 128]
    ksend[...] = kf[...].astype(BF)

    pl.semaphore_wait(barrier, 31 + 4 * len(near) + 2)

    for copy in fetched[3:]:
        copy.wait()

    def first(slot, step, xx):
        return remote(ksend.at[xx], kraw.at[slot, x], ks_sem.at[slot, xx], kr_sem.at[slot, x], along_z(step, xx))

    def first_came(slot, step, xx):
        remote(ksend.at[xx], kraw.at[slot, xx], ks_sem.at[slot, xx], kr_sem.at[slot, xx], along_z(step, xx)).wait_recv()

    for slot, step in enumerate(near):
        for d in (2, 1, 3, 0):
            first(slot, step, (x + d) % 4).start()
    for d in range(1, 4):
        first(4, 0, (x + d) % 4).start()
    kraw[4, x] = ksend[x]

    def rows_of(mm):
        return modes_ref.at[pl.ds(mm * 8, 8)]

    fs[...] = jnp.ones_like(fs)
    fs[0:18, 0:64] = freq_ref[...]
    for d in range(1, 8):
        mm = (me + d) % 8
        remote(rows_of(mm), mrecv.at[me], ms_sem.at[mm], mr_sem.at[me], at(x, mm)).start()
        remote(fs, frecv.at[me], fs_sem.at[mm], fr_sem.at[me], at(x, mm)).start()
    own_modes = pltpu.make_async_copy(rows_of(me), mrecv.at[me], c_sem.at[4])
    own_modes.start()
    frecv[me] = fs[...]

    qs[...] = jnp.zeros_like(qs)
    qs[0:3, 0:64] = qp_ref[...].astype(F32)
    points = dot_t(first_ref[...], qs[...].astype(BF)).astype(BF)
    inner = dot(points, lattice_ref[...]).astype(jnp.int32) & 31
    angle = inner.astype(F32) * (TWO_PI / 32)
    ph[x, 0:64, :] = jnp.cos(angle).astype(BF)
    ph[x, 64:128, :] = jnp.sin(angle).astype(BF)

    def hop(offset, step, part):
        spot = (offset - step) % nz
        piece = kbuf.at[(z + nz + offset) % nz, pl.ds(part * 144, 144)]
        return remote(piece, piece, zs_sem.at[spot, part], zr_sem.at[spot, part], along_z(step))

    def came(offset, part):
        hop(offset, 0, part).wait_recv()

    def assemble(slot, step):
        for xx in range(4):
            first_came(slot, step, xx)
        kbuf[(z + nz - step) % nz] = dot(gather_ref[...], kraw[slot].reshape(320, 128)).astype(BF)

    routes = {-3: (3, 1, -1), 3: (-3, 1, -1), -6: (1, -1), 6: (1, -1)}

    for d in range(1, 4):
        xx = (x + d) % 4
        remote(ph.at[x], ph.at[x], ps_sem.at[xx], pr_sem.at[x], at(xx, me)).start()

    @pl.loop(0, 32, unroll=4)
    def _(i):
        both = [rotq_ref[pl.ds(pl.multiple_of(ri * 1024 + i * 32, 32), 32), :] for ri in range(2)]
        flipped = dot_t(second_ref[...], jnp.concatenate(both, axis=0))
        for q4 in range(4):
            xf[q4, pl.ds(i, 16, stride=32), :] = flipped[q4 * 16:(q4 + 1) * 16]

    assemble(0, 3)
    assemble(1, -3)
    for part in range(2):
        hop(-3, 3, part).start()
        hop(3, -3, part).start()
    for part in range(2):
        for offset in (-3, 3):
            for step in (1, -1):
                hop(offset, step, part).start()

    lane_m = lax.broadcasted_iota(jnp.int32, (256, 128), 1) % 16
    for t in range(8):
        chosen = jnp.where((shift_ref[...] == ws_ref[t]) & (lane_m < wc_ref[t]), 1.0, 0.0).astype(BF)
        cut = jnp.zeros((64, 128), F32)
        for q4 in range(4):
            cut = cut + dot(xf[q4, t * 64:(t + 1) * 64, :].astype(BF), chosen[q4 * 64:(q4 + 1) * 64])
        win[x, 0, t * 32:(t + 1) * 32, :] = cut[0:32].astype(BF)
        win[x, 1, t * 32:(t + 1) * 32, :] = cut[32:64].astype(BF)
    for d in range(1, 4):
        xx = (x + d) % 4
        remote(win.at[x], win.at[x], ns_sem.at[xx], nr_sem.at[x], at(xx, me)).start()

    def weights(xx):
        for par in range(2):
            for q4 in range(4):
                spreaded = dot(win[xx, par], spread_ref[par, :, q4 * 512:(q4 + 1) * 512]).astype(BF)
                for g in range(4):
                    rows = spreaded[:, g * 128:(g + 1) * 128].reshape(8, 32, 128)
                    start = par * 128 + g * 32
                    wq[pl.ds(xx * 8, 8), q4, start:start + 32, :] = rows

    row_q = sum((lax.broadcasted_iota(jnp.int32, (144, 128), 0) >= 18 * n).astype(jnp.int32) for n in range(1, 8))
    diagonal = lax.broadcasted_iota(jnp.int32, (144, 128), 1) == row_q + me * 8

    def vectors(mm):
        own = 1.0 / jnp.sqrt(2.0 * frecv[mm])
        high = own.astype(BF)
        rest = own - high.astype(F32)
        middle = rest.astype(BF)
        low = (rest - middle.astype(F32)).astype(BF)
        by_row = dot(rowmode_ref[...], high) + dot(rowmode_ref[...], middle) + dot(rowmode_ref[...], low)
        scale[mm] = jnp.sum(jnp.where(diagonal, by_row, 0.0), axis=1, keepdims=True)
        rows = mrecv[mm].reshape(288, 144)
        mf[0] = rows[:, :128].astype(F32)
        mf[1, :, 0:16] = rows[:, 128:].astype(F32)
        for ri in range(2):
            halves = [mf[n, pl.ds(ri, 144, stride=2), :].astype(BF) for n in range(2)]
            spreaded = dot(jnp.concatenate(halves, axis=1), pick_ref[...])
            for par in range(2):
                own_rows = spreaded[par * 72:(par + 1) * 72] * mask_ref[...]
                lhs[par, mm, 0:72, ri * 640:(ri + 1) * 640] = own_rows.astype(BF)

    def wait_window(xx):
        remote(win.at[xx], win.at[xx], ns_sem.at[xx], nr_sem.at[xx], at(xx, me)).wait_recv()

    def wait_vectors(mm):
        remote(rows_of(mm), mrecv.at[mm], ms_sem.at[mm], mr_sem.at[mm], at(x, mm)).wait_recv()
        remote(fs, frecv.at[mm], fs_sem.at[mm], fr_sem.at[mm], at(x, mm)).wait_recv()

    for copy in constant[:3]:
        copy.wait()
    own_modes.wait()
    weights(x)
    for part in range(2):
        for offset in (-6, 6):
            came(offset, part)
            for step in (1, -1):
                hop(offset, step, part).start()
            if (offset, part) in ((-6, 0), (6, 1)):
                hop(offset, 2 if part == 0 else -2, part).start()
    vectors(me)
    for d in range(1, 4):
        wait_window((x + d) % 4)
        weights((x + d) % 4)
    for d in range(1, 8):
        wait_vectors((me + d) % 8)
        vectors((me + d) % 8)
    for d in range(1, 4):
        first_came(4, 0, (x + d) % 4)
    kbuf[z] = dot(gather_ref[...], kraw[4].reshape(320, 128)).astype(BF)
    assemble(2, 1)
    assemble(3, -1)
    for offset in (-2, 2, -4, 4, -5, 5, -7, 7, 8):
        for part in range(2):
            came(offset, part)

    for d in range(1, 4):
        xx = (x + d) % 4
        remote(ph.at[xx], ph.at[xx], ps_sem.at[xx], pr_sem.at[xx], at(xx, me)).wait_recv()
    turn = lax.broadcasted_iota(jnp.int32, (64, 128), 1) < 64

    def sums(xx):
        for cp in range(9):
            pair = [kbuf[:, (cp * 2 + p) * 16:(cp * 2 + p) * 16 + 16, :].reshape(nr, 128) for p in range(2)]
            both = dot(ph[xx], jnp.concatenate(pair, axis=1))
            for p in range(2):
                along = both[0:64, p * 128:(p + 1) * 128]
                across = pltpu.roll(both[64:128, p * 128:(p + 1) * 128], 64, 1)
                total = along + jnp.where(turn, -across, across)
                for par in range(2):
                    qbuf[par, pl.ds(xx * 640 + cp * 2 + p, 32, stride=20), :] = total[par * 32:(par + 1) * 32]

    row = lax.broadcasted_iota(jnp.int32, (80, 256), 0)

    def band(xx, mm):
        spot = xx * 8 + mm
        rows = pl.ds(pl.multiple_of(spot * 80, 80), 80)
        own = jnp.concatenate([qbuf[0, rows, :], qbuf[1, rows, :]], axis=1)
        wide = [
            jnp.where((row >= q4 * 20) & (row < q4 * 20 + 20), own, 0.0).astype(BF) for q4 in range(4)
        ]
        return dot(jnp.concatenate(wide, axis=1), wq[spot].reshape(1024, 128)).astype(BF)

    def block(xx, mm, sx, sm):
        return remote(
            bsend.at[xx * 8 + mm], brecv.at[sx, sm], bs_sem.at[xx * 8 + mm], br_sem.at[sx * 8 + sm], at(xx, mm)
        )

    @pl.loop(0, 3)
    def _(n):
        xx = (x + 2 - n + n // 2 * 3) % 4
        sums(xx)
        for half in range(2):
            for mm in range(half * 4, half * 4 + 4):
                bsend[xx * 8 + mm] = band(xx, mm)
            for mm in range(half * 4, half * 4 + 4):
                block(xx, mm, x, me).start()

    sums(x)
    for d in range(1, 8):
        bsend[x * 8 + (me + d) % 8] = band(x, (me + d) % 8)
        block(x, (me + d) % 8, x, me).start()
    brecv[x, me] = band(x, me)

    constant[3].wait()
    for d in (0, 1, 3, 2):
        xx = (x + d) % 4

        @pl.loop(1 if d == 0 else 0, 8)
        def _(n):
            block(xx, (me + n) % 8, xx, (me + n) % 8).wait_recv()

        placed = dot(brecv[xx].reshape(640, 128), order_ref[pl.ds(pl.multiple_of(xx * 128, 128), 128), :]).astype(BF)
        for part in range(4):
            here = placed[:, part * 256:(part + 1) * 256]
            if d > 0:
                here = here + rhs[part * 640:(part + 1) * 640, :]
            rhs[part * 640:(part + 1) * 640, :] = here

    def finish(chip):
        for par in range(2):
            done = dot(lhs[par, pl.ds(chip * 2, 2)].reshape(160, 1280), rhs[par * 1280:(par + 1) * 1280, :])
            for n in range(2):
                one = done[n * 80:n * 80 + 72] * scale[chip * 2 + n, par * 72:(par + 1) * 72]
                for ri in range(2):
                    of[n, pl.ds(par * 144 + ri, 72, stride=2), :] = one[:, ri * 128:(ri + 1) * 128]
        for n in range(2):
            osend[chip * 2 + n] = of[n].astype(BF)

    def send_out(mm):
        remote(osend.at[mm], o_ref.at[me], os_sem.at[mm], or_sem.at[me], at(x, mm)).start()

    for d in (2, 1, 3):
        chip = (me // 2 + d) % 4
        finish(chip)
        send_out(chip * 2 + me % 2)
        send_out(chip * 2 + 1 - me % 2)
    finish(me // 2)
    send_out(me // 2 * 2 + 1 - me % 2)
    o_ref[me] = osend[me]

    @pl.loop(1, 8)
    def _(d):
        mm = (me + d) % 8
        remote(osend.at[mm], o_ref.at[mm], os_sem.at[mm], or_sem.at[mm], at(x, mm)).wait()

    for slot, step in enumerate(near):
        for xx in range(4):
            first(slot, step, xx).wait_send()
    for d in range(1, 4):
        xx = (x + d) % 4
        first(4, 0, xx).wait_send()
        remote(ph.at[x], ph.at[x], ps_sem.at[xx], pr_sem.at[x], at(xx, me)).wait_send()
        remote(win.at[x], win.at[x], ns_sem.at[xx], nr_sem.at[x], at(xx, me)).wait_send()
    for d in range(1, 8):
        mm = (me + d) % 8
        remote(rows_of(mm), mrecv.at[me], ms_sem.at[mm], mr_sem.at[me], at(x, mm)).wait_send()
        remote(fs, frecv.at[me], fs_sem.at[mm], fr_sem.at[me], at(x, mm)).wait_send()
    for part in range(2):
        for offset, steps in routes.items():
            for step in steps:
                hop(offset, step, part).wait_send()
    hop(-6, 2, 0).wait_send()
    hop(6, -2, 1).wait_send()

    @pl.loop(1, 32)
    def _(d):
        xx, mm = (x + d // 8) % 4, (me + d) % 8
        block(xx, mm, x, me).wait_send()


def shards(g_wann, rot_k, qpoints, rot_kq, win_count, win_start, modes_vec, frequencies):
    nz = lax.axis_size("pb") // NX
    small, large = constants(nz)

    g_rows = g_wann.reshape(4, 2, 18, 8, 128).transpose(0, 2, 3, 1, 4).reshape(1152, 128)
    rot = rot_k.transpose(0, 2, 1)
    rotq = rot_kq.transpose(1, 2, 3, 0).reshape(2048, 64)
    freq = frequencies.T
    modes = modes_vec.transpose(0, 2, 1, 3)

    vmem = pl.BlockSpec(memory_space=pltpu.VMEM)
    whole = pl.BlockSpec(memory_space=pl.ANY)
    sem = pltpu.SemaphoreType.DMA
    out = pl.pallas_call(
        functools.partial(kernel, nz),
        out_shape=jax.ShapeDtypeStruct((8, 288, 128), BF),
        in_specs=[whole] * 19,
        out_specs=vmem,
        scratch_shapes=[
            pltpu.SMEM((8,), jnp.int32), pltpu.SMEM((8,), jnp.int32),
            *[pltpu.VMEM(a.shape, a.dtype) for a in (g_rows, rot, qpoints, rotq, freq, *small)],
            pltpu.VMEM((2, 128, 2048), BF),
            pltpu.VMEM((256, 640), BF),
            pltpu.VMEM((72, 640), F32),
            pltpu.VMEM((512, 1024), BF),
            pltpu.VMEM((1152, 128), F32),
            pltpu.VMEM((80, 2048), BF),
            pltpu.VMEM((2048, 512), BF),
            pltpu.VMEM((80, 512), F32),
            pltpu.VMEM((8, 128), F32),
            pltpu.VMEM((24, 128), F32),
            pltpu.VMEM((4, 80, 128), F32),
            pltpu.VMEM((4, 80, 128), BF),
            pltpu.VMEM((5, 4, 80, 128), BF),
            pltpu.VMEM((nz, 288, 128), BF),
            pltpu.VMEM((4, 128, nz * 16), BF),
            pltpu.VMEM((4, 512, 64), F32),
            pltpu.VMEM((4, 2, 256, 128), BF),
            pltpu.VMEM((32, 4, 256, 128), BF),
            pltpu.VMEM((2, 2560, 128), F32),
            pltpu.VMEM((32, 80, 128), BF),
            pltpu.VMEM((4, 8, 80, 128), BF),
            pltpu.VMEM((8, 8, 18, 2, 144), BF),
            pltpu.VMEM((2, 288, 128), F32),
            pltpu.VMEM((8, 24, 128), F32),
            pltpu.VMEM((2, 8, 80, 1280), BF),
            pltpu.VMEM((8, 144, 1), F32),
            pltpu.VMEM((2560, 256), BF),
            pltpu.VMEM((2, 288, 128), F32),
            pltpu.VMEM((8, 288, 128), BF),
            sem((5,)), sem((14,)),
            sem((5, 4)), sem((5, 4)), sem((4,)), sem((4,)), sem((4,)), sem((4,)), sem((8,)), sem((8,)), sem((8,)), sem((8,)),
            sem((16, 2)), sem((16, 2)), sem((32,)), sem((32,)), sem((8,)), sem((8,)),
        ],
        compiler_params=pltpu.CompilerParams(
            collective_id=0, has_side_effects=True, vmem_limit_bytes=56 * 1024 * 1024
        ),
    )(win_start, win_count, g_rows, rot, qpoints, rotq, freq, modes, *small, *large)
    return out.reshape(64, 18, 2, 128).transpose(0, 2, 1, 3)


def solution(mesh):
    placed = (
        P("pb", None, "mode", None),
        P(),
        P(None, "pb"),
        P("pb", None, None, None),
        P("pb"),
        P("pb"),
        P("pb", None, "mode", None),
        P("pb", "mode"),
    )
    return jax.shard_map(
        shards, mesh=mesh, in_specs=placed, out_specs=P("pb", None, "mode", None), check_vma=False
    )
```

```python
import functools
import jax
import jax.numpy as jnp
import numpy as np
from jax import lax
from jax.experimental import pallas as pl
from jax.experimental.pallas import tpu as pltpu
from jax.sharding import PartitionSpec as P

NX = 4
NM = 8
TWO_PI = 6.283185307179586
BF = jnp.bfloat16
F32 = jnp.float32


def dot(a, b):
    return jnp.dot(a, b, preferred_element_type=F32)


def dot_t(a, b):
    return lax.dot_general(a, b, (((1,), (1,)), ((), ())), preferred_element_type=F32)


def constants(nz):
    rows = np.arange(nz * 16)
    z, x, r4 = rows // 16, rows // 4 % 4, rows % 4
    r = (x * nz + z) * 4 + r4
    lattice = np.zeros((8, nz * 16), np.float32)
    lattice[0] = r % 8 - 4
    lattice[1] = r // 8 % 8 - 4
    lattice[2] = r // 64 - 4

    row, lane = np.arange(256)[:, None], np.arange(128)[None, :]
    same = row // 32 == lane // 16
    shift = np.where(same, row % 32 - lane % 16, -1000).astype(np.int32)

    spread = np.zeros((2, 4, 2, 16, 4, 2, 2, 2, 2, 16, 2), np.float32)
    for par in range(2):
        for q4 in range(4):
            for m in range(16):
                for b in range(2):
                    spread[par, q4, 0, m, q4, 0, b, par, 0, m, b] = 1
                    spread[par, q4, 1, m, q4, 1, b, par, 0, m, b] = 1
                    spread[par, q4, 1, m, q4, 0, b, par, 1, m, b] = -1
                    spread[par, q4, 0, m, q4, 1, b, par, 1, m, b] = 1
    spread = spread.reshape(2, 128, 2048)

    pick = np.zeros((256, 640), np.float32)
    for c in range(144):
        for q4 in range(4):
            pick[c, c // 18 * 80 + q4 * 20 + c % 18] = 1
    mask = np.zeros((4, 18, 8, 4, 20), np.float32)
    for q4 in range(4):
        mask[q4, :, :, q4, :] = 1
    mask = mask.reshape(72, 640)

    order = np.zeros((4, 2, 2, 16, 2, 2, 2, 2, 16, 8), np.float32)
    for xx in range(4):
        for par in range(2):
            for m in range(16):
                for b in range(2):
                    order[xx, par, 0, m, b, par, 0, 0, m, xx * 2 + b] = 1
                    order[xx, par, 1, m, b, par, 0, 1, m, xx * 2 + b] = 1
                    order[xx, par, 1, m, b, par, 1, 0, m, xx * 2 + b] = -1
                    order[xx, par, 0, m, b, par, 1, 1, m, xx * 2 + b] = 1
    order = order.reshape(512, 1024)

    bands = np.zeros((8, 4, 2, 2, 32), np.float32)
    for xx in range(4):
        for b in range(2):
            bands[xx * 2 + b, xx, :, b, :] = 1
    bands = bands.reshape(8, 512)

    q = np.arange(64)
    first = np.zeros((64, 128), np.float32)
    first[q, q // 4 % 8 * 8 + q // 32 * 4 + q % 4] = 1
    second = np.zeros((64, 64), np.float32)
    second[q, q // 2 % 8 * 8 + q % 2 * 4 + q // 16] = 1

    gather = np.zeros((18, 4, 4, 4, 80), np.float32)
    for c in range(18):
        for xx in range(4):
            for r4 in range(4):
                gather[c, xx, r4, xx, c * 4 + r4] = 1
    gather = gather.reshape(288, 320)

    modes = np.zeros((144, 24), np.float32)
    modes[np.arange(144), np.arange(144) % 18] = 1
    half = lambda a: jnp.asarray(a, BF)
    small = [half(lattice), jnp.asarray(shift), half(bands), half(first), half(second), half(modes), half(gather)]
    return small, [half(spread), half(pick), jnp.asarray(mask), half(order)]


def kernel(
    nz, ws_in, wc_in, g_in, rot_in, qp_in, rotq_in, freq_in, modes_ref,
    lattice_in, shift_in, bands_in, first_in, second_in, rowmode_in, gather_in, spread_in, pick_in, mask_in, order_in,
    o_ref,
    ws_ref, wc_ref, g_ref, rot_ref, qp_ref, rotq_ref, freq_ref,
    lattice_ref, shift_ref, bands_ref, first_ref, second_ref, rowmode_ref, gather_ref,
    spread_ref, pick_ref, mask_ref, order_ref,
    gf, gl, kw, tf, qs, fs, kf, ksend, kraw, kbuf, ph, xf, win, wq, qbuf, bsend, brecv, mrecv, mf, frecv, lhs, scale, rhs,
    of, osend, c_sem, i_sem,
    ks_sem, kr_sem, ps_sem, pr_sem, ns_sem, nr_sem, ms_sem, mr_sem, fs_sem, fr_sem, zs_sem, zr_sem, bs_sem, br_sem,
    os_sem, or_sem,
):
    me = lax.axis_index("mode")
    pb = lax.axis_index("pb")
    x, z = pb // nz, pb % nz
    nr = nz * 16

    def at(xx, mm):
        return {"mode": mm, "pb": xx * nz + z}

    def remote(src, dst, ssem, rsem, where):
        return pltpu.make_async_remote_copy(
            src_ref=src, dst_ref=dst, send_sem=ssem, recv_sem=rsem,
            device_id=where, device_id_type=pl.DeviceIdType.MESH,
        )

    def along_z(step, xx=None):
        return {"mode": me, "pb": (x if xx is None else xx) * nz + (z + nz + step) % nz}

    barrier = pltpu.get_barrier_semaphore()

    @pl.loop(1, 32)
    def _(d):
        pl.semaphore_signal(
            barrier, inc=1, device_id=at((x + d // 8) % 4, (me + d) % 8), device_id_type=pl.DeviceIdType.MESH
        )

    near = (3, -3, 1, -1)
    for step in near:
        for xx in range(4):
            pl.semaphore_signal(barrier, inc=1, device_id=along_z(step, xx), device_id_type=pl.DeviceIdType.MESH)
    for step in (2, -2):
        pl.semaphore_signal(barrier, inc=1, device_id=along_z(step), device_id_type=pl.DeviceIdType.MESH)

    fetched = [
        pltpu.make_async_copy(source, held, i_sem.at[n])
        for n, (source, held) in enumerate(
            (
                (rot_in, rot_ref), (bands_in, bands_ref), (g_in, g_ref), (ws_in, ws_ref), (wc_in, wc_ref),
                (qp_in, qp_ref), (rotq_in, rotq_ref), (freq_in, freq_ref), (lattice_in, lattice_ref),
                (shift_in, shift_ref), (first_in, first_ref), (second_in, second_ref), (rowmode_in, rowmode_ref),
                (gather_in, gather_ref),
            )
        )
    ]
    for copy in fetched:
        copy.start()
    constant = [
        pltpu.make_async_copy(source, held, c_sem.at[n])
        for n, (source, held) in enumerate(
            ((spread_in, spread_ref), (pick_in, pick_ref), (mask_in, mask_ref), (order_in, order_ref))
        )
    ]
    for copy in fetched[:2]:
        copy.wait()
    lane = lax.broadcasted_iota(jnp.int32, (32, 512), 1)
    lane_i = lane % 32
    turn_b = lambda ri: lax.dot_general(
        rot_ref[ri], bands_ref[...], (((0,), (0,)), ((), ())), preferred_element_type=F32
    )
    real, imag = turn_b(0), turn_b(1)
    in_real = lane % 128 < 64
    parts = (jnp.where(in_real, real, imag).astype(BF), jnp.where(in_real, -imag, real).astype(BF))
    for ri in range(2):
        part = parts[ri]

        @pl.loop(0, 32, unroll=4)
        def _(i):
            kw[pl.ds(pl.multiple_of(ri * 1024 + i * 32, 32), 32), :] = jnp.where(lane_i == i, part, 0.0).astype(BF)

    fetched[2].wait()
    gf[...] = g_ref[...].astype(F32)
    for ri in range(2):
        for k in range(8):
            block = (ri * 8 + k) * 128
            gl[0:72, block:block + 128] = gf[pl.ds(k * 2 + ri, 72, stride=16), :].astype(BF)
    tf[...] = dot(gl[...], kw[...])
    kf[...] = jnp.zeros_like(kf)
    for xx in range(4):
        for r in range(4):
            kf[xx, pl.ds(r, 18, stride=4), :] = tf[r * 18:r * 18 + 18, xx * 128:(xx + 1) * 128]
    ksend[...] = kf[...].astype(BF)

    pl.semaphore_wait(barrier, 31 + 4 * len(near) + 2)

    def first(slot, step, xx):
        return remote(ksend.at[xx], kraw.at[slot, x], ks_sem.at[slot, xx], kr_sem.at[slot, x], along_z(step, xx))

    def first_came(slot, step, xx):
        remote(ksend.at[xx], kraw.at[slot, xx], ks_sem.at[slot, xx], kr_sem.at[slot, xx], along_z(step, xx)).wait_recv()

    for slot, step in enumerate(near):
        for d in (2, 1, 3, 0):
            first(slot, step, (x + d) % 4).start()
    for d in range(1, 4):
        first(4, 0, (x + d) % 4).start()
    kraw[4, x] = ksend[x]
    for copy in constant:
        copy.start()
    for copy in fetched[3:]:
        copy.wait()
    qbuf[...] = jnp.zeros_like(qbuf)
    mf[...] = jnp.zeros_like(mf)

    def rows_of(mm):
        return modes_ref.at[pl.ds(mm * 8, 8)]

    fs[...] = jnp.ones_like(fs)
    fs[0:18, 0:64] = freq_ref[...]
    for d in range(1, 8):
        mm = (me + d) % 8
        remote(rows_of(mm), mrecv.at[me], ms_sem.at[mm], mr_sem.at[me], at(x, mm)).start()
        remote(fs, frecv.at[me], fs_sem.at[mm], fr_sem.at[me], at(x, mm)).start()
    own_modes = pltpu.make_async_copy(rows_of(me), mrecv.at[me], c_sem.at[4])
    own_modes.start()
    frecv[me] = fs[...]

    qs[...] = jnp.zeros_like(qs)
    qs[0:3, 0:64] = qp_ref[...].astype(F32)
    points = dot_t(first_ref[...], qs[...].astype(BF)).astype(BF)
    inner = dot(points, lattice_ref[...]).astype(jnp.int32) & 31
    angle = inner.astype(F32) * (TWO_PI / 32)
    ph[x, 0:64, :] = jnp.cos(angle).astype(BF)
    ph[x, 64:128, :] = jnp.sin(angle).astype(BF)

    def hop(offset, step, part):
        spot = (offset - step) % nz
        piece = kbuf.at[(z + nz + offset) % nz, pl.ds(part * 144, 144)]
        return remote(piece, piece, zs_sem.at[spot, part], zr_sem.at[spot, part], along_z(step))

    def came(offset, part):
        hop(offset, 0, part).wait_recv()

    def assemble(slot, step):
        for xx in range(4):
            first_came(slot, step, xx)
        kbuf[(z + nz - step) % nz] = dot(gather_ref[...], kraw[slot].reshape(320, 128)).astype(BF)

    routes = {-3: (3, 1, -1), 3: (-3, 1, -1), -6: (1, -1), 6: (1, -1)}

    for d in range(1, 4):
        xx = (x + d) % 4
        remote(ph.at[x], ph.at[x], ps_sem.at[xx], pr_sem.at[x], at(xx, me)).start()

    @pl.loop(0, 32, unroll=4)
    def _(i):
        both = [rotq_ref[pl.ds(pl.multiple_of(ri * 1024 + i * 32, 32), 32), :] for ri in range(2)]
        flipped = dot_t(second_ref[...], jnp.concatenate(both, axis=0))
        for q4 in range(4):
            xf[q4, pl.ds(i, 16, stride=32), :] = flipped[q4 * 16:(q4 + 1) * 16]

    for slot, step in ((0, 3), (1, -3)):
        assemble(slot, step)
        for part in range(2):
            hop(-step, step, part).start()
    for part in range(2):
        for offset in (-3, 3):
            for step in (1, -1):
                hop(offset, step, part).start()

    lane_m = lax.broadcasted_iota(jnp.int32, (256, 128), 1) % 16
    for t in range(8):
        chosen = jnp.where((shift_ref[...] == ws_ref[t]) & (lane_m < wc_ref[t]), 1.0, 0.0).astype(BF)
        cut = jnp.zeros((64, 128), F32)
        for q4 in range(4):
            cut = cut + dot(xf[q4, t * 64:(t + 1) * 64, :].astype(BF), chosen[q4 * 64:(q4 + 1) * 64])
        win[x, 0, t * 32:(t + 1) * 32, :] = cut[0:32].astype(BF)
        win[x, 1, t * 32:(t + 1) * 32, :] = cut[32:64].astype(BF)
    for d in range(1, 4):
        xx = (x + d) % 4
        remote(win.at[x], win.at[x], ns_sem.at[xx], nr_sem.at[x], at(xx, me)).start()

    def weights(xx):
        for par in range(2):
            for q4 in range(4):
                spreaded = dot(win[xx, par], spread_ref[par, :, q4 * 512:(q4 + 1) * 512]).astype(BF)
                for g in range(4):
                    rows = spreaded[:, g * 128:(g + 1) * 128].reshape(8, 32, 128)
                    start = par * 128 + g * 32
                    wq[pl.ds(xx * 8, 8), q4, start:start + 32, :] = rows

    row_q = sum((lax.broadcasted_iota(jnp.int32, (144, 128), 0) >= 18 * n).astype(jnp.int32) for n in range(1, 8))
    diagonal = lax.broadcasted_iota(jnp.int32, (144, 128), 1) == row_q + me * 8

    def vectors(mm):
        own = 1.0 / jnp.sqrt(2.0 * frecv[mm])
        high = own.astype(BF)
        rest = own - high.astype(F32)
        middle = rest.astype(BF)
        low = (rest - middle.astype(F32)).astype(BF)
        by_row = dot(rowmode_ref[...], high) + dot(rowmode_ref[...], middle) + dot(rowmode_ref[...], low)
        scale[mm] = jnp.sum(jnp.where(diagonal, by_row, 0.0), axis=1, keepdims=True)
        rows = mrecv[mm].reshape(288, 144)
        mf[0] = rows[:, :128].astype(F32)
        mf[1, :, 0:16] = rows[:, 128:].astype(F32)
        for ri in range(2):
            halves = [mf[n, pl.ds(ri, 144, stride=2), :].astype(BF) for n in range(2)]
            spreaded = dot(jnp.concatenate(halves, axis=1), pick_ref[...])
            for par in range(2):
                own_rows = spreaded[par * 72:(par + 1) * 72] * mask_ref[...]
                lhs[par, mm, 0:72, ri * 640:(ri + 1) * 640] = own_rows.astype(BF)

    def wait_window(xx):
        remote(win.at[xx], win.at[xx], ns_sem.at[xx], nr_sem.at[xx], at(xx, me)).wait_recv()

    def wait_vectors(mm):
        remote(rows_of(mm), mrecv.at[mm], ms_sem.at[mm], mr_sem.at[mm], at(x, mm)).wait_recv()
        remote(fs, frecv.at[mm], fs_sem.at[mm], fr_sem.at[mm], at(x, mm)).wait_recv()

    for copy in constant[:3]:
        copy.wait()
    own_modes.wait()
    weights(x)
    for part in range(2):
        for offset in (-6, 6):
            came(offset, part)
            for step in (1, -1):
                hop(offset, step, part).start()
            if (offset, part) in ((-6, 0), (6, 1)):
                hop(offset, 2 if part == 0 else -2, part).start()
    for d in range(1, 4):
        first_came(4, 0, (x + d) % 4)
    kbuf[z] = dot(gather_ref[...], kraw[4].reshape(320, 128)).astype(BF)
    assemble(2, 1)
    assemble(3, -1)
    vectors(me)
    for d in range(1, 4):
        wait_window((x + d) % 4)
        weights((x + d) % 4)
    for d in range(1, 8):
        wait_vectors((me + d) % 8)
        vectors((me + d) % 8)
    for offset in (-2, 2, -4, 4, -5, 5, -7, 7, 8):
        for part in range(2):
            came(offset, part)

    for d in range(1, 4):
        xx = (x + d) % 4
        remote(ph.at[xx], ph.at[xx], ps_sem.at[xx], pr_sem.at[xx], at(xx, me)).wait_recv()
    turn = lax.broadcasted_iota(jnp.int32, (64, 128), 1) < 64

    def sums(xx):
        for cp in range(9):
            pair = [kbuf[:, (cp * 2 + p) * 16:(cp * 2 + p) * 16 + 16, :].reshape(nr, 128) for p in range(2)]
            both = dot(ph[xx], jnp.concatenate(pair, axis=1))
            for p in range(2):
                along = both[0:64, p * 128:(p + 1) * 128]
                across = pltpu.roll(both[64:128, p * 128:(p + 1) * 128], 64, 1)
                total = along + jnp.where(turn, -across, across)
                for par in range(2):
                    qbuf[par, pl.ds(xx * 640 + cp * 2 + p, 32, stride=20), :] = total[par * 32:(par + 1) * 32]

    row = lax.broadcasted_iota(jnp.int32, (80, 256), 0)

    def band(xx, mm):
        spot = xx * 8 + mm
        rows = pl.ds(pl.multiple_of(spot * 80, 80), 80)
        own = jnp.concatenate([qbuf[0, rows, :], qbuf[1, rows, :]], axis=1)
        wide = [
            jnp.where((row >= q4 * 20) & (row < q4 * 20 + 20), own, 0.0).astype(BF) for q4 in range(4)
        ]
        return dot(jnp.concatenate(wide, axis=1), wq[spot].reshape(1024, 128)).astype(BF)

    def block(xx, mm, sx, sm):
        return remote(
            bsend.at[xx * 8 + mm], brecv.at[sx, sm], bs_sem.at[xx * 8 + mm], br_sem.at[sx * 8 + sm], at(xx, mm)
        )

    @pl.loop(0, 3)
    def _(n):
        xx = (x + 2 - n + n // 2 * 3) % 4
        sums(xx)
        for half in range(4):
            for mm in range(half * 2, half * 2 + 2):
                bsend[xx * 8 + mm] = band(xx, mm)
            for mm in range(half * 2, half * 2 + 2):
                block(xx, mm, x, me).start()

    sums(x)
    for d in range(1, 8):
        bsend[x * 8 + (me + d) % 8] = band(x, (me + d) % 8)
        block(x, (me + d) % 8, x, me).start()
    brecv[x, me] = band(x, me)

    constant[3].wait()
    for d in (0, 1, 3, 2):
        xx = (x + d) % 4

        @pl.loop(1 if d == 0 else 0, 8)
        def _(n):
            block(xx, (me + n) % 8, xx, (me + n) % 8).wait_recv()

        placed = dot(brecv[xx].reshape(640, 128), order_ref[pl.ds(pl.multiple_of(xx * 128, 128), 128), :]).astype(BF)
        for part in range(4):
            here = placed[:, part * 256:(part + 1) * 256]
            if d > 0:
                here = here + rhs[part * 640:(part + 1) * 640, :]
            rhs[part * 640:(part + 1) * 640, :] = here

    def finish(chip):
        for par in range(2):
            done = dot(lhs[par, pl.ds(chip * 2, 2)].reshape(160, 1280), rhs[par * 1280:(par + 1) * 1280, :])
            for n in range(2):
                one = done[n * 80:n * 80 + 72] * scale[chip * 2 + n, par * 72:(par + 1) * 72]
                for ri in range(2):
                    of[n, pl.ds(par * 144 + ri, 72, stride=2), :] = one[:, ri * 128:(ri + 1) * 128]
        for n in range(2):
            osend[chip * 2 + n] = of[n].astype(BF)

    def send_out(mm):
        remote(osend.at[mm], o_ref.at[me], os_sem.at[mm], or_sem.at[me], at(x, mm)).start()

    for d in (2, 1, 3):
        chip = (me // 2 + d) % 4
        finish(chip)
        send_out(chip * 2 + me % 2)
        send_out(chip * 2 + 1 - me % 2)
    finish(me // 2)
    send_out(me // 2 * 2 + 1 - me % 2)
    o_ref[me] = osend[me]

    @pl.loop(1, 8)
    def _(d):
        mm = (me + d) % 8
        remote(osend.at[mm], o_ref.at[mm], os_sem.at[mm], or_sem.at[mm], at(x, mm)).wait()

    for slot, step in enumerate(near):
        for xx in range(4):
            first(slot, step, xx).wait_send()
    for d in range(1, 4):
        xx = (x + d) % 4
        first(4, 0, xx).wait_send()
        remote(ph.at[x], ph.at[x], ps_sem.at[xx], pr_sem.at[x], at(xx, me)).wait_send()
        remote(win.at[x], win.at[x], ns_sem.at[xx], nr_sem.at[x], at(xx, me)).wait_send()
    for d in range(1, 8):
        mm = (me + d) % 8
        remote(rows_of(mm), mrecv.at[me], ms_sem.at[mm], mr_sem.at[me], at(x, mm)).wait_send()
        remote(fs, frecv.at[me], fs_sem.at[mm], fr_sem.at[me], at(x, mm)).wait_send()
    for part in range(2):
        for offset, steps in routes.items():
            for step in steps:
                hop(offset, step, part).wait_send()
    hop(-6, 2, 0).wait_send()
    hop(6, -2, 1).wait_send()

    @pl.loop(1, 32)
    def _(d):
        xx, mm = (x + d // 8) % 4, (me + d) % 8
        block(xx, mm, x, me).wait_send()


def shards(g_wann, rot_k, qpoints, rot_kq, win_count, win_start, modes_vec, frequencies):
    nz = lax.axis_size("pb") // NX
    small, large = constants(nz)

    g_rows = g_wann.reshape(4, 2, 18, 8, 128).transpose(0, 2, 3, 1, 4).reshape(1152, 128)
    rot = rot_k.transpose(0, 2, 1)
    rotq = rot_kq.transpose(1, 2, 3, 0).reshape(2048, 64)
    freq = frequencies.T
    modes = modes_vec.transpose(0, 2, 1, 3)

    vmem = pl.BlockSpec(memory_space=pltpu.VMEM)
    whole = pl.BlockSpec(memory_space=pl.ANY)
    sem = pltpu.SemaphoreType.DMA
    out = pl.pallas_call(
        functools.partial(kernel, nz),
        out_shape=jax.ShapeDtypeStruct((8, 288, 128), BF),
        in_specs=[whole] * 19,
        out_specs=vmem,
        scratch_shapes=[
            pltpu.SMEM((8,), jnp.int32), pltpu.SMEM((8,), jnp.int32),
            *[pltpu.VMEM(a.shape, a.dtype) for a in (g_rows, rot, qpoints, rotq, freq, *small)],
            pltpu.VMEM((2, 128, 2048), BF),
            pltpu.VMEM((256, 640), BF),
            pltpu.VMEM((72, 640), F32),
            pltpu.VMEM((512, 1024), BF),
            pltpu.VMEM((1152, 128), F32),
            pltpu.VMEM((80, 2048), BF),
            pltpu.VMEM((2048, 512), BF),
            pltpu.VMEM((80, 512), F32),
            pltpu.VMEM((8, 128), F32),
            pltpu.VMEM((24, 128), F32),
            pltpu.VMEM((4, 80, 128), F32),
            pltpu.VMEM((4, 80, 128), BF),
            pltpu.VMEM((5, 4, 80, 128), BF),
            pltpu.VMEM((nz, 288, 128), BF),
            pltpu.VMEM((4, 128, nz * 16), BF),
            pltpu.VMEM((4, 512, 64), F32),
            pltpu.VMEM((4, 2, 256, 128), BF),
            pltpu.VMEM((32, 4, 256, 128), BF),
            pltpu.VMEM((2, 2560, 128), F32),
            pltpu.VMEM((32, 80, 128), BF),
            pltpu.VMEM((4, 8, 80, 128), BF),
            pltpu.VMEM((8, 8, 18, 2, 144), BF),
            pltpu.VMEM((2, 288, 128), F32),
            pltpu.VMEM((8, 24, 128), F32),
            pltpu.VMEM((2, 8, 80, 1280), BF),
            pltpu.VMEM((8, 144, 1), F32),
            pltpu.VMEM((2560, 256), BF),
            pltpu.VMEM((2, 288, 128), F32),
            pltpu.VMEM((8, 288, 128), BF),
            sem((5,)), sem((14,)),
            sem((5, 4)), sem((5, 4)), sem((4,)), sem((4,)), sem((4,)), sem((4,)), sem((8,)), sem((8,)), sem((8,)), sem((8,)),
            sem((16, 2)), sem((16, 2)), sem((32,)), sem((32,)), sem((8,)), sem((8,)),
        ],
        compiler_params=pltpu.CompilerParams(
            collective_id=0, has_side_effects=True, vmem_limit_bytes=56 * 1024 * 1024
        ),
    )(win_start, win_count, g_rows, rot, qpoints, rotq, freq, modes, *small, *large)
    return out.reshape(64, 18, 2, 128).transpose(0, 2, 1, 3)


def solution(mesh):
    placed = (
        P("pb", None, "mode", None),
        P(),
        P(None, "pb"),
        P("pb", None, None, None),
        P("pb"),
        P("pb"),
        P("pb", None, "mode", None),
        P("pb", "mode"),
    )
    return jax.shard_map(
        shards, mesh=mesh, in_specs=placed, out_specs=P("pb", None, "mode", None), check_vma=False
    )
```
